256 devices in a mesh: blk: 64 (over z, x, core), grp: 4 (over y).
Axes of the slice: x: 4, y: 4, z: 8, core: 2. Of those that a mesh axis runs over, the one named last changes fastest.
Arguments:
- embeddings: bfloat16 [768, 1024, 1024], P(('blk', 'grp'))
- ranks: int32 [768, 1024], P(('blk', 'grp')), may hold values from 0 to 1048575
- block_rows: int32 [768], P(('blk', 'grp')), may hold values from 1 to 1024, as said below
- pair_list: int32 [256, 6, 2], P(('blk', 'grp')), may hold values from 1 to 5, as said below
- pair_count: int32 [256], P(('blk', 'grp')), may hold values from 1 to 6, as said below
Outputs:
- best: float32 [768, 1024], P(('blk', 'grp'))
The draws below stay inside these ranges and needn't reach their ends.
Inputs may be any that keep to these rules, and one draw needn't show every extreme that they name: `block_rows`: A block that is not the last of its cluster has 1024 live rows. `pair_list`: the blocks fall into clusters of 1 to 3 consecutive blocks, some of exactly 3. The first pair_count entries of a device are (u, v) with 3 <= u < 6 and u - 3 < v <= u, naming two blocks of one cluster or a block with itself; over all devices they name every such pair of a cluster once, at the device of the later block; the other entries are (3, 3). `pair_count`: some device has 6 live slots.
All inputs are finite; a program needn't handle non-finite values.
Results may differ from the reference program's by a relative error of at most 0.0003.
Values may be sent and summed in bfloat16 or wider, within the bound.
No kernel may reach another device: no remote copies, remote signals or barrier semaphores. Data moves between devices by JAX's collectives and lax.ppermute only.
A program may use at most 128 MiB of HBM per device.

```python
import math
import jax
import jax.numpy as jnp
from jax import lax

D = 1024
BLK = 1024
BPD = 3
PAIRS = 6
BLOCKS = 768


def cluster_layout(key):
    lengths = jax.random.randint(jax.random.fold_in(key, 101), (BLOCKS,), 1, BPD + 1)
    lengths = lengths.at[0].set(1).at[1].set(BPD)
    ends = jnp.cumsum(lengths)
    starts = ends - lengths
    marks = jnp.zeros((BLOCKS + 1,), jnp.int32).at[jnp.minimum(starts, BLOCKS)].set(1)
    cluster_index = (jnp.cumsum(marks[:BLOCKS]) - 1).astype(jnp.int32)
    first_block = starts[cluster_index].astype(jnp.int32)
    span_blocks = lengths[cluster_index].astype(jnp.int32)
    label = (jnp.minimum(ends[cluster_index], BLOCKS) - 1).astype(jnp.int32)
    return (label, first_block, span_blocks)


def pair_layout(key):
    cluster, first_block, span_blocks = cluster_layout(key)
    device_count = BLOCKS // BPD
    blocks = jnp.arange(BLOCKS).reshape(device_count, BPD)
    depth = blocks - first_block.reshape(device_count, BPD)
    inner = jnp.arange(BPD)[None, :, None]
    offset = jnp.arange(BPD)[None, None, :]
    valid = offset <= depth[:, :, None]
    first_pos = jnp.broadcast_to(BPD + inner, valid.shape)
    second_pos = first_pos - offset
    keys = jnp.where(valid, 0, 1) * (BPD * BPD) + inner * BPD + offset
    keys = keys.reshape(device_count, BPD * BPD)
    ordering = jnp.argsort(keys, axis=-1)[:, :PAIRS]
    valid_flat = jnp.take_along_axis(valid.reshape(device_count, BPD * BPD), ordering, axis=-1)
    first_flat = jnp.take_along_axis(first_pos.reshape(device_count, BPD * BPD), ordering, axis=-1)
    second_flat = jnp.take_along_axis(second_pos.reshape(device_count, BPD * BPD), ordering, axis=-1)
    first_flat = jnp.where(valid_flat, first_flat, BPD)
    second_flat = jnp.where(valid_flat, second_flat, BPD)
    listing = jnp.stack([first_flat, second_flat], axis=-1).astype(jnp.int32)
    counts = jnp.sum(valid.reshape(device_count, BPD * BPD), axis=-1).astype(jnp.int32)
    return (listing, counts)


def draw_block_rows(key, part):
    cluster, first_block, span_blocks = cluster_layout(key)
    key = jax.random.fold_in(key, 7)
    last_one = jnp.arange(BLOCKS) - first_block + 1 == span_blocks
    partial_rows = jax.random.randint(key, (BLOCKS,), 1, BLK + 1)
    return jnp.where(last_one, partial_rows, BLK).astype(jnp.int32)


def draw_pair_list(key, part):
    listing, counts = pair_layout(key)
    return listing


def draw_pair_count(key, part):
    listing, counts = pair_layout(key)
    return counts


def draw_embeddings(key, part):
    cluster, first_block, span_blocks = cluster_layout(key)
    key = jax.random.fold_in(key, 5)
    keys = jax.random.split(key, 6)
    center = 0.7 * jnp.clip(jax.random.normal(keys[0], (BLOCKS, D), jnp.float32), -5.0, 5.0)
    noise = jnp.clip(jax.random.normal(keys[1], (BLOCKS, BLK, D), jnp.float32), -5.0, 5.0)
    center = center[cluster]
    source = first_block + jax.random.randint(keys[2], (BLOCKS,), 0, span_blocks)
    source = source.at[BPD].set(1)
    rolling = jax.random.randint(keys[3], (BLOCKS,), 1, BLK)
    row_index = (jnp.arange(BLK)[None, :] + rolling[:, None]) % BLK
    partner = noise[source[:, None], row_index]
    copied = jax.random.bernoulli(keys[4], 0.5, (BLOCKS, BLK))
    content = jnp.where(copied[:, :, None], partner + 0.25 * noise, noise)
    scaling = jnp.exp(jax.random.uniform(keys[5], (BLOCKS, BLK, 1), jnp.float32, 0.0, math.log(10.0)))
    return (scaling * (center[:, None, :] + content)).astype(jnp.bfloat16)


def place_ends(drawn, own_key, smallest, top_value):
    longest = drawn.shape.index(max(drawn.shape))
    spots = []
    for shift in (0, 1):
        where = [jax.random.randint(jax.random.fold_in(own_key, axis), (), 0, length) for axis, length in enumerate(drawn.shape)]
        where[longest] = (where[longest] + shift) % drawn.shape[longest]
        spots.append(tuple(where))
    return drawn.at[spots[0]].set(smallest).at[spots[1]].set(top_value)


def setup_inputs(seed: int = 0) -> dict:
    seeds = jax.random.split(jax.random.key(seed), 6)
    embeddings = draw_embeddings(jax.random.fold_in(seeds[5], 71), 0)
    ranks = place_ends(jax.random.randint(seeds[1], (BLOCKS, BLK), 0, 1048576), jax.random.fold_in(seeds[1], 1), 0, 1048575).astype(jnp.int32)
    block_rows = draw_block_rows(jax.random.fold_in(seeds[5], 71), 0)
    pair_list = draw_pair_list(jax.random.fold_in(seeds[5], 71), 0)
    pair_count = draw_pair_count(jax.random.fold_in(seeds[5], 71), 0)
    return dict(embeddings=embeddings, ranks=ranks, block_rows=block_rows, pair_list=pair_list, pair_count=pair_count)


def reference(embeddings, ranks, block_rows, pair_list, pair_count):
    values = embeddings.astype(jnp.float32)
    scaling = lax.rsqrt(lax.optimization_barrier(jnp.sum(values * values, axis=-1, keepdims=True)) + 1e-06)
    unit_rows = (values * scaling).astype(jnp.bfloat16)
    live_rows = jnp.arange(BLK)[None, :] < block_rows[:, None]
    device_count = pair_list.shape[0]
    slot_total = device_count * PAIRS
    flat_pairs = pair_list.reshape(slot_total, 2)
    owners = (jnp.arange(slot_total) // PAIRS).astype(jnp.int32)
    slot_ids = (jnp.arange(slot_total) % PAIRS).astype(jnp.int32)

    def visit(best_rows, item):
        owner, slot_id, first_pos, second_pos = item
        taken = slot_id < pair_count[owner]
        first_block = jnp.clip(owner * BPD + first_pos - BPD, 0, BLOCKS - 1).astype(jnp.int32)
        second_block = jnp.clip(owner * BPD + second_pos - BPD, 0, BLOCKS - 1).astype(jnp.int32)
        left_rows = unit_rows[first_block].astype(jnp.float32)
        right_rows = unit_rows[second_block].astype(jnp.float32)
        similarity = jnp.dot(left_rows, right_rows.T, precision=lax.Precision.HIGHEST)
        shifted = 1.0 + similarity
        paired = live_rows[first_block][:, None] & live_rows[second_block][None, :]
        paired = paired & taken
        rank_left = ranks[first_block][:, None]
        rank_right = ranks[second_block][None, :]
        row_best = lax.optimization_barrier(jnp.max(jnp.where(paired & (rank_right < rank_left), shifted, 0.0), axis=1))
        col_best = lax.optimization_barrier(jnp.max(jnp.where(paired & (rank_left < rank_right), shifted, 0.0), axis=0))
        best_rows = best_rows.at[first_block].max(row_best)
        best_rows = best_rows.at[second_block].max(col_best)
        return (best_rows, None)
    start_rows = jnp.zeros((BLOCKS, BLK), jnp.float32)
    best_rows, _ = lax.scan(visit, start_rows, (owners, slot_ids, flat_pairs[:, 0], flat_pairs[:, 1]))
    return best_rows
```

```python
import functools

import jax
import jax.numpy as jnp
from jax import lax
from jax.experimental import pallas as pl
from jax.experimental.pallas import tpu as pltpu
from jax.sharding import PartitionSpec as P

ROWS = 1024
DIM = 1024
HELD = 3
TILE = 256
LANES = 128
NONE = -1e30
DEAD = 1 << 30
AXES = ("blk", "grp")
CUTS = (0, 256, 768, 1024)


def passed_along(value, steps):
    count = lax.axis_size(AXES)
    leading, last = (max(0, -steps), min(count, count - steps))
    return lax.ppermute(value, AXES, [(source, source + steps) for source in range(leading, last)])


def unit_rows(raw):
    values = raw.astype(jnp.float32)
    scaling = lax.rsqrt(jnp.sum(values * values, axis=-1, keepdims=True) + 1e-06)
    return (values * scaling).astype(jnp.bfloat16)


def spread(keys_row):
    return jnp.broadcast_to(keys_row, (LANES, LANES)).T


def gathered(partial):
    return jnp.max(partial.T, axis=0, keepdims=True)


def pair_tile(left_units, left_keys, right_units, right_keys):
    similarity = lax.dot_general(
        left_units, right_units, (((1,), (1,)), ((), ())), preferred_element_type=jnp.float32
    )
    rows, cols = similarity.shape
    left_best = None
    right_best = []
    for group in range(cols // LANES):
        part = similarity[:, group * LANES : (group + 1) * LANES]
        keys = right_keys[:, group * LANES : (group + 1) * LANES]
        for_left = jnp.where(keys < left_keys, part, NONE)
        left_best = for_left if left_best is None else jnp.maximum(left_best, for_left)
        for_right = jnp.where(left_keys < keys, part, NONE)
        right_best.append(jnp.max(for_right.reshape(rows // 8, 8, LANES), axis=0))
    return left_best, jnp.concatenate(right_best, axis=1)


def local_kernel(pairs, count, raw, keys, units, best, spread_keys, left_acc, right_acc):
    for block in range(HELD):
        for group in range(ROWS // LANES):
            rows = pl.ds(group * LANES, LANES)
            spread_keys[block, rows, :] = spread(keys[block : block + 1, rows])

    def normalize(step, carry):
        block, rows = step // (ROWS // LANES), pl.ds((step % (ROWS // LANES)) * LANES, LANES)
        units[block, rows, :] = unit_rows(raw[block, rows, :])
        return carry

    lax.fori_loop(0, HELD * ROWS // LANES, normalize, 0)
    left_acc[...] = jnp.full_like(left_acc, NONE)
    right_acc[...] = jnp.full_like(right_acc, NONE)

    def visit(slot, carry):
        left, right = pairs[2 * slot], pairs[2 * slot + 1]

        @pl.when(right >= HELD)
        def _():
            def step(index, carry):
                rows = pl.ds((index // (ROWS // TILE)) * TILE, TILE)
                cols = pl.ds((index % (ROWS // TILE)) * TILE, TILE)
                left_best, right_best = pair_tile(
                    units[left - HELD, rows, :],
                    spread_keys[left - HELD, rows, :],
                    units[right - HELD, cols, :],
                    keys[pl.ds(right - HELD, 1), cols],
                )
                left_acc[left - HELD, rows, :] = jnp.maximum(left_acc[left - HELD, rows, :], left_best)
                right_acc[right - HELD, :, cols] = jnp.maximum(right_acc[right - HELD, :, cols], right_best)
                return carry

            lax.fori_loop(0, (ROWS // TILE) ** 2, step, 0)

        return carry

    lax.fori_loop(0, count[0], visit, 0)
    for block in range(HELD):
        for group in range(ROWS // LANES):
            rows = pl.ds(group * LANES, LANES)
            found = jnp.maximum(
                gathered(left_acc[block, rows, :]),
                jnp.max(right_acc[block, :, rows], axis=0, keepdims=True),
            )
            best[block : block + 1, rows] = jnp.maximum(1.0 + found, 0.0)


def local_pairs(pair_list, pair_count, embeddings, keys):
    smem, vmem = pl.BlockSpec(memory_space=pltpu.SMEM), pl.BlockSpec(memory_space=pltpu.VMEM)
    return pl.pallas_call(
        local_kernel,
        out_shape=(
            jax.ShapeDtypeStruct((HELD, ROWS, DIM), jnp.bfloat16),
            jax.ShapeDtypeStruct((HELD, ROWS), jnp.float32),
        ),
        in_specs=[smem, smem, vmem, vmem],
        out_specs=(vmem, vmem),
        scratch_shapes=[
            pltpu.VMEM((HELD, ROWS, LANES), jnp.int32),
            pltpu.VMEM((HELD, ROWS, LANES), jnp.float32),
            pltpu.VMEM((HELD, 8, ROWS), jnp.float32),
        ],
        compiler_params=pltpu.CompilerParams(vmem_limit_bytes=32 << 20),
        cost_estimate=pl.CostEstimate(flops=6 * 2 * ROWS * ROWS * DIM, bytes_accessed=4 * HELD * ROWS * DIM, transcendentals=0),
    )(pair_list.reshape(-1), pair_count, embeddings, keys)


def arrival_kernel(partners, flags, *refs):
    raws = refs[:-8]
    guest_keys, keys, units, guest_best, best, guest_units, left_acc, right_acc = refs[-8:]
    rows_in_all = sum(raw.shape[0] for raw in raws)
    left_acc[...] = jnp.full_like(left_acc, NONE)
    right_acc[...] = jnp.full_like(right_acc, NONE)

    @pl.when((flags[0] != 0) | (flags[1] != 0))
    def _():
        first = 0
        for raw in raws:
            def normalize(step, carry, raw=raw, first=first):
                start = pl.multiple_of(step * LANES, LANES)
                guest_units[pl.ds(first + start, LANES), :] = unit_rows(raw[pl.ds(start, LANES), :])
                return carry

            lax.fori_loop(0, raw.shape[0] // LANES, normalize, 0)
            first += raw.shape[0]

        for which, block in enumerate(partners):
            @pl.when(flags[which] != 0)
            def _(which=which, block=block):
                def step(index, carry):
                    start = pl.multiple_of((index // (ROWS // TILE)) * TILE, TILE)
                    rows, cols = pl.ds(start, TILE), pl.ds((index % (ROWS // TILE)) * TILE, TILE)
                    spread_keys = jnp.concatenate(
                        [spread(guest_keys[:, pl.ds(start + part * LANES, LANES)]) for part in range(TILE // LANES)], axis=0
                    )
                    left_best, right_best = pair_tile(
                        guest_units[rows, :], spread_keys, units[block, cols, :], keys[block : block + 1, cols]
                    )
                    left_acc[rows, :] = jnp.maximum(left_acc[rows, :], left_best)
                    right_acc[which, :, cols] = jnp.maximum(right_acc[which, :, cols], right_best)
                    return carry

                lax.fori_loop(0, rows_in_all // TILE * (ROWS // TILE), step, 0)

    for group in range(rows_in_all // LANES):
        rows = pl.ds(group * LANES, LANES)
        guest_best[:, rows] = jnp.maximum(1.0 + gathered(left_acc[rows, :]), 0.0)
    for which, block in enumerate(partners):
        found = jnp.max(right_acc[which], axis=0, keepdims=True)
        best[which : which + 1, :] = jnp.maximum(1.0 + found, 0.0)


def arrival_pairs(partners, flags, raws, guest_keys, keys, units):
    smem, vmem = pl.BlockSpec(memory_space=pltpu.SMEM), pl.BlockSpec(memory_space=pltpu.VMEM)
    rows = sum(raw.shape[0] for raw in raws)
    return pl.pallas_call(
        functools.partial(arrival_kernel, partners),
        out_shape=(
            jax.ShapeDtypeStruct((1, rows), jnp.float32),
            jax.ShapeDtypeStruct((2, ROWS), jnp.float32),
        ),
        in_specs=[smem] + [vmem] * (len(raws) + 3),
        out_specs=(vmem, vmem),
        scratch_shapes=[
            pltpu.VMEM((rows, DIM), jnp.bfloat16),
            pltpu.VMEM((rows, LANES), jnp.float32),
            pltpu.VMEM((2, 8, ROWS), jnp.float32),
        ],
        compiler_params=pltpu.CompilerParams(vmem_limit_bytes=32 << 20),
        cost_estimate=pl.CostEstimate(
            flops=2 * 2 * rows * ROWS * DIM, bytes_accessed=2 * (rows + HELD * ROWS) * DIM, transcendentals=0
        ),
    )(flags, *raws, guest_keys, keys, units)


def local(embeddings, ranks, block_rows, pair_list, pair_count):
    pieces = list(zip(CUTS[:-1], CUTS[1:]))
    keys = jnp.where(jnp.arange(ROWS)[None, :] < block_rows[:, None], ranks, DEAD)
    taken = jnp.arange(pair_list.shape[1]) < pair_count[0]
    listed = lambda u, v: jnp.any(taken & (pair_list[0, :, 0] == u) & (pair_list[0, :, 1] == v)).astype(jnp.int32)
    ahead = listed(HELD + 1, HELD - 1)
    left_flags = jnp.stack([ahead * listed(HELD, HELD - 1), ahead])
    sent_flags = jnp.stack([(1 - ahead) * listed(HELD, HELD - 1), listed(HELD, HELD - 2)])
    note = jnp.concatenate([keys[0], sent_flags, jnp.zeros((LANES - 2,), jnp.int32)])

    from_before, from_after = [], []
    for index, (low, high) in enumerate(pieces):
        if index == len(pieces) - 1:
            keys_before = passed_along(keys[HELD - 1], 1)
            note_after = passed_along(note, -1)
        from_before.append(passed_along(embeddings[HELD - 1, low:high], 1))
        from_after.append(passed_along(embeddings[0, low:high], -1))
    keys_before = keys_before[None, :]
    keys_after = note_after[None, :ROWS]
    right_flags = note_after[ROWS : ROWS + 2]

    units, best = local_pairs(pair_list, pair_count, embeddings, keys)

    split = CUTS[-2]
    before_early, best_before_early = arrival_pairs((0, 1), left_flags, from_before[:-1], keys_before[:, :split], keys, units)
    after_early, best_after_early = arrival_pairs((2, 1), right_flags, from_after[:-1], keys_after[:, :split], keys, units)
    before_late, best_before_late = arrival_pairs((0, 1), left_flags, from_before[-1:], keys_before[:, split:], keys, units)
    back = passed_along(jnp.concatenate([before_early, before_late], axis=1), -1)
    after_late, best_after_late = arrival_pairs((2, 1), right_flags, from_after[-1:], keys_after[:, split:], keys, units)
    onward = passed_along(jnp.concatenate([after_early, after_late], axis=1), 1)

    best_before = jnp.maximum(best_before_early, best_before_late)
    best_after = jnp.maximum(best_after_early, best_after_late)
    found = jnp.stack(
        [
            jnp.maximum(best_before[0], onward[0]),
            jnp.maximum(best_before[1], best_after[1]),
            jnp.maximum(best_after[0], back[0]),
        ]
    )
    return jnp.where(keys != DEAD, jnp.maximum(best, found), 0.0)


def solution(mesh):
    in_specs = (
        P(AXES, None, None),
        P(AXES, None),
        P(AXES),
        P(AXES, None, None),
        P(AXES),
    )
    return jax.shard_map(local, mesh=mesh, in_specs=in_specs, out_specs=P(AXES, None), check_vma=False)
```

```python
import functools

import jax
import jax.numpy as jnp
from jax import lax
from jax.experimental import pallas as pl
from jax.experimental.pallas import tpu as pltpu
from jax.sharding import PartitionSpec as P

ROWS = 1024
DIM = 1024
HELD = 3
COLS = 256
LANES = 128
NOTE = 16
EARLY = 768
LATE = ROWS - EARLY
DIGIT = 128
DEAD = DIGIT**3 - 1
NONE = -1e30
AXES = ("blk", "grp")
SMEM = pl.BlockSpec(memory_space=pltpu.SMEM)
VMEM = pl.BlockSpec(memory_space=pltpu.VMEM)
HBM = pl.BlockSpec(memory_space=pltpu.HBM)


def passed_along(value, steps):
    count = lax.axis_size(AXES)
    leading, last = (max(0, -steps), min(count, count - steps))
    return lax.ppermute(value, AXES, [(source, source + steps) for source in range(leading, last)])


def shaped(shape, dtype):
    return jax.ShapeDtypeStruct(shape, dtype)


def unit_rows(raw):
    values = raw.astype(jnp.float32)
    scaling = lax.rsqrt(jnp.sum(values * values, axis=-1, keepdims=True) + 1e-06)
    return (values * scaling).astype(jnp.bfloat16)


def normalize(raw, units, rows):
    def step(index, carry):
        at = pl.ds(pl.multiple_of(index * LANES, LANES), LANES)
        units[at, :] = unit_rows(raw[at, :])
        return carry

    lax.fori_loop(0, rows // LANES, step, 0, unroll=2)


def spread(keys_row):
    return jnp.broadcast_to(keys_row, (LANES, LANES)).T


def gathered(partial):
    return jnp.max(partial.T, axis=0, keepdims=True)


def shifted(found):
    return jnp.maximum(1.0 + found, 0.0)


def pair_tile(left_units, left_keys, right_units, right_keys):
    similarity = lax.dot_general(
        left_units, right_units, (((1,), (1,)), ((), ())), preferred_element_type=jnp.float32
    )
    rows, cols = similarity.shape
    left_best = None
    right_best = []
    for group in range(cols // LANES):
        part = similarity[:, group * LANES : (group + 1) * LANES]
        keys = right_keys[:, group * LANES : (group + 1) * LANES]
        for_left = jnp.where(keys < left_keys, part, NONE)
        left_best = for_left if left_best is None else jnp.maximum(left_best, for_left)
        for_right = jnp.where(left_keys < keys, part, NONE)
        right_best.append(jnp.max(for_right.reshape(rows // 8, 8, LANES), axis=0))
    return left_best, jnp.concatenate(right_best, axis=1)


def pair_strip(first, left_units, left_keys, left_acc, right_units, right_keys, right_acc, cols):
    rows = pl.ds(first, left_units.shape[0] - first)
    left_best, right_best = pair_tile(left_units[rows, :], left_keys[rows, :], right_units[cols, :], right_keys[:, cols])
    left_acc[rows, :] = jnp.maximum(left_acc[rows, :], left_best)
    right_acc[:, cols] = jnp.maximum(right_acc[:, cols], right_best)


def note_rows(keys, flags):
    row = lax.broadcasted_iota(jnp.int32, (NOTE, ROWS), 0)
    values = [keys % DIGIT, (keys // DIGIT) % DIGIT, keys // DIGIT**2] + flags
    note = jnp.zeros((NOTE, ROWS), jnp.int32)
    for index, value in enumerate(values):
        note = jnp.where(row == index, value, note)
    return note.astype(jnp.float32).astype(jnp.bfloat16)


def noted_keys(note):
    digits = note.astype(jnp.float32).astype(jnp.int32)
    return digits[0:1] + digits[1:2] * DIGIT + digits[2:3] * DIGIT**2


def early_kernel(pairs, count, live, ranks, raw, onward, back, keys, flags, sems):
    copies = [
        pltpu.make_async_copy(raw.at[block, pl.ds(0, EARLY)], piece.at[pl.ds(0, EARLY)], sems.at[index])
        for index, (block, piece) in enumerate(((HELD - 1, onward), (0, back)))
    ]
    for copy in copies:
        copy.start()
    position = lax.broadcasted_iota(jnp.int32, (1, ROWS), 1)
    for block in range(HELD):
        keys[block : block + 1, :] = jnp.where(position < live[block], ranks[block : block + 1, :], DEAD)

    def listed(u, v):
        found = jnp.int32(0)
        for slot in range(pairs.shape[2]):
            hit = (slot < count[0]) & (pairs[0, 0, slot] == u) & (pairs[0, 1, slot] == v)
            found = found | hit.astype(jnp.int32)
        return found

    ahead, near, far = listed(HELD + 1, HELD - 1), listed(HELD, HELD - 1), listed(HELD, HELD - 2)
    flags[0] = ahead * near
    flags[1] = ahead
    onward[pl.ds(EARLY, NOTE), :] = note_rows(keys[HELD - 1 : HELD, :], [])
    back[pl.ds(EARLY, NOTE), :] = note_rows(keys[0:1, :], [(1 - ahead) * near, far])
    for copy in copies:
        copy.wait()


def early_pieces(pairs, count, live, ranks, raw):
    piece = shaped((EARLY + NOTE, DIM), jnp.bfloat16)
    return pl.pallas_call(
        early_kernel,
        out_shape=(piece, piece, shaped((HELD, ROWS), jnp.int32), shaped((2,), jnp.int32)),
        in_specs=[SMEM, SMEM, SMEM, VMEM, HBM],
        out_specs=(VMEM, VMEM, VMEM, SMEM),
        scratch_shapes=[pltpu.SemaphoreType.DMA((2,))],
        compiler_params=pltpu.CompilerParams(vmem_limit_bytes=6 << 20),
        cost_estimate=pl.CostEstimate(flops=0, bytes_accessed=8 * EARLY * DIM, transcendentals=0),
    )(pairs, count, live, ranks, raw)


def late_kernel(flags, raw, onward, back, flags_again, sems):
    copies = [
        pltpu.make_async_copy(raw.at[block, pl.ds(EARLY, LATE)], piece, sems.at[index])
        for index, (block, piece) in enumerate(((HELD - 1, onward), (0, back)))
    ]
    for copy in copies:
        copy.start()
    flags_again[0] = flags[0]
    flags_again[1] = flags[1]
    for copy in copies:
        copy.wait()


def late_pieces(flags, raw):
    piece = shaped((LATE, DIM), jnp.bfloat16)
    return pl.pallas_call(
        late_kernel,
        out_shape=(piece, piece, shaped((2,), jnp.int32)),
        in_specs=[SMEM, HBM],
        out_specs=(VMEM, VMEM, SMEM),
        scratch_shapes=[pltpu.SemaphoreType.DMA((2,))],
        compiler_params=pltpu.CompilerParams(vmem_limit_bytes=4 << 20),
        cost_estimate=pl.CostEstimate(flops=0, bytes_accessed=8 * LATE * DIM, transcendentals=0),
    )(flags, raw)


def local_kernel(pairs, count, flags, raw, keys, units, best, spread_keys, left_acc, right_acc):
    for block in range(HELD):
        for group in range(ROWS // LANES):
            rows = pl.ds(group * LANES, LANES)
            spread_keys[block, rows, :] = spread(keys[block : block + 1, rows])
        normalize(raw.at[block], units.at[block], ROWS)
    left_acc[...] = jnp.full_like(left_acc, NONE)
    right_acc[...] = jnp.full_like(right_acc, NONE)

    def visit(slot, carry):
        left, right = pairs[0, 0, slot] - HELD, pairs[0, 1, slot] - HELD

        def strip(first, col):
            pair_strip(
                first, units.at[left], spread_keys.at[left], left_acc.at[left],
                units.at[right], keys.at[pl.ds(right, 1)], right_acc.at[right], pl.ds(col, COLS),
            )

        @pl.when(right == left)
        def _():
            for col in range(0, ROWS, COLS):
                strip(col, col)

        @pl.when((right >= 0) & (right != left))
        def _():
            for col in range(0, ROWS, COLS):
                strip(0, col)

        return carry

    lax.fori_loop(0, count[0], visit, 0)
    for block in range(HELD):
        for group in range(ROWS // LANES):
            rows = pl.ds(group * LANES, LANES)
            found = jnp.maximum(
                gathered(left_acc[block, rows, :]),
                jnp.max(right_acc[block, :, rows], axis=0, keepdims=True),
            )
            best[block : block + 1, rows] = shifted(found)


def local_pairs(pairs, count, flags, raw, keys):
    return pl.pallas_call(
        local_kernel,
        out_shape=(shaped((HELD, ROWS, DIM), jnp.bfloat16), shaped((HELD, ROWS), jnp.float32)),
        in_specs=[SMEM, SMEM, SMEM, VMEM, VMEM],
        out_specs=(VMEM, VMEM),
        scratch_shapes=[
            pltpu.VMEM((HELD, ROWS, LANES), jnp.int32),
            pltpu.VMEM((HELD, ROWS, LANES), jnp.float32),
            pltpu.VMEM((HELD, 8, ROWS), jnp.float32),
        ],
        compiler_params=pltpu.CompilerParams(vmem_limit_bytes=24 << 20),
        cost_estimate=pl.CostEstimate(flops=6 * 2 * ROWS * ROWS * DIM, bytes_accessed=4 * HELD * ROWS * DIM, transcendentals=0),
    )(pairs, count, flags, raw, keys)


def guest_pairs(flags, block_of, guest_rows, raw, guest_keys, keys, units, guest_units, spread_keys, left_acc, right_acc):
    left_acc[...] = jnp.full_like(left_acc, NONE)

    @pl.when((flags[0] != 0) | (flags[1] != 0))
    def _():
        normalize(raw, guest_units, guest_rows)
        for group in range(guest_rows // LANES):
            rows = pl.ds(group * LANES, LANES)
            spread_keys[rows, :] = spread(guest_keys[:, group * LANES : (group + 1) * LANES])

        def visit(which, carry):
            block = block_of(which)

            @pl.when(flags[which] != 0)
            def _():
                for col in range(0, ROWS, COLS):
                    pair_strip(
                        0, guest_units, spread_keys, left_acc,
                        units.at[block], keys.at[pl.ds(block, 1)], right_acc.at[block], pl.ds(col, COLS),
                    )

            return carry

        lax.fori_loop(0, 2, visit, 0)


def finish(left_acc, guest_best, first, right_acc, best_before, best):
    for group in range(left_acc.shape[0] // LANES):
        rows = pl.ds(group * LANES, LANES)
        guest_best[:, pl.ds(first + group * LANES, LANES)] = shifted(gathered(left_acc[rows, :]))
    if best is not None:
        for block in range(HELD):
            found = jnp.max(right_acc[block], axis=0, keepdims=True)
            best[block : block + 1, :] = jnp.maximum(best_before[block : block + 1, :], shifted(found))


def from_before(which):
    return which


def from_after(which):
    return HELD - 1 - which


def middle_kernel(
    flags, raw_before, raw_after, keys, units, best_before,
    guest_before, guest_after, best, keys_before, keys_after, flags_after,
    guest_units, spread_keys, left_acc, right_acc,
):
    keys_before[...] = noted_keys(raw_before[pl.ds(EARLY, NOTE), :])
    note = raw_after[pl.ds(EARLY, NOTE), :]
    keys_after[...] = noted_keys(note)
    for which in range(2):
        flags_after[which] = (jnp.max(note[3 + which : 4 + which, :].astype(jnp.float32)) > 0.5).astype(jnp.int32)
    right_acc[...] = jnp.full_like(right_acc, NONE)
    common = (keys, units, guest_units, spread_keys, left_acc, right_acc)
    guest_pairs(flags, from_before, EARLY, raw_before, keys_before[:, :EARLY], *common)
    finish(left_acc, guest_before, 0, right_acc, None, None)
    guest_pairs(flags_after, from_after, EARLY, raw_after, keys_after[:, :EARLY], *common)
    finish(left_acc, guest_after, 0, right_acc, best_before, best)


def guest_scratch(rows):
    return [
        pltpu.VMEM((rows, DIM), jnp.bfloat16),
        pltpu.VMEM((rows, LANES), jnp.int32),
        pltpu.VMEM((rows, LANES), jnp.float32),
        pltpu.VMEM((HELD, 8, ROWS), jnp.float32),
    ]


def middle_pairs(flags, raw_before, raw_after, keys, units, best_before):
    row = shaped((1, ROWS), jnp.int32)
    guest = shaped((1, EARLY), jnp.float32)
    return pl.pallas_call(
        middle_kernel,
        out_shape=(guest, guest, shaped((HELD, ROWS), jnp.float32), row, row, shaped((2,), jnp.int32)),
        in_specs=[SMEM] + [VMEM] * 5,
        out_specs=(VMEM,) * 5 + (SMEM,),
        scratch_shapes=guest_scratch(EARLY),
        compiler_params=pltpu.CompilerParams(vmem_limit_bytes=18 << 20),
        cost_estimate=pl.CostEstimate(flops=6 * EARLY * ROWS * DIM, bytes_accessed=2 * (2 * EARLY + HELD * ROWS) * DIM, transcendentals=0),
    )(flags, raw_before, raw_after, keys, units, best_before)


def last_kernel(
    block_of, flags, raw, guest_keys, keys, units, guest_early, best_before, guest_best, best,
    guest_units, spread_keys, left_acc, right_acc,
):
    right_acc[...] = jnp.full_like(right_acc, NONE)
    guest_pairs(flags, block_of, LATE, raw, guest_keys[:, EARLY:], keys, units, guest_units, spread_keys, left_acc, right_acc)
    guest_best[:, pl.ds(0, EARLY)] = guest_early[...]
    finish(left_acc, guest_best, EARLY, right_acc, best_before, best)


def last_pairs(block_of, flags, raw, guest_keys, keys, units, guest_early, best_before):
    return pl.pallas_call(
        functools.partial(last_kernel, block_of),
        out_shape=(shaped((1, ROWS), jnp.float32), shaped((HELD, ROWS), jnp.float32)),
        in_specs=[SMEM] + [VMEM] * 6,
        out_specs=(VMEM, VMEM),
        scratch_shapes=guest_scratch(LATE),
        compiler_params=pltpu.CompilerParams(vmem_limit_bytes=12 << 20),
        cost_estimate=pl.CostEstimate(flops=4 * LATE * ROWS * DIM, bytes_accessed=2 * (LATE + HELD * ROWS) * DIM, transcendentals=0),
    )(flags, raw, guest_keys, keys, units, guest_early, best_before)


def local(embeddings, ranks, block_rows, pair_list, pair_count):
    pairs = pair_list.transpose(0, 2, 1)
    early_on, early_back, keys, flags = early_pieces(pairs, pair_count, block_rows, ranks, embeddings)
    late_on, late_back, flags = late_pieces(flags, embeddings)
    early_before, early_after = passed_along(early_on, 1), passed_along(early_back, -1)
    late_before, late_after = passed_along(late_on, 1), passed_along(late_back, -1)
    units, best = local_pairs(pairs, pair_count, flags, embeddings, keys)
    guest_before, guest_after, best, keys_before, keys_after, flags_after = middle_pairs(
        flags, early_before, early_after, keys, units, best
    )
    returned, best = last_pairs(from_before, flags, late_before, keys_before, keys, units, guest_before, best)
    back = passed_along(returned, -1)
    returned, best = last_pairs(from_after, flags_after, late_after, keys_after, keys, units, guest_after, best)
    onward = passed_along(returned, 1)
    found = jnp.concatenate([onward, jnp.zeros_like(onward), back], axis=0)
    return jnp.where(keys != DEAD, jnp.maximum(best, found), 0.0)


def solution(mesh):
    in_specs = (
        P(AXES, None, None),
        P(AXES, None),
        P(AXES),
        P(AXES, None, None),
        P(AXES),
    )
    return jax.shard_map(local, mesh=mesh, in_specs=in_specs, out_specs=P(AXES, None), check_vma=False)
```

```python
import functools

import jax
import jax.numpy as jnp
from jax import lax
from jax.experimental import pallas as pl
from jax.experimental.pallas import tpu as pltpu
from jax.sharding import PartitionSpec as P

ROWS = 1024
DIM = 1024
HELD = 3
COLS = 256
LANES = 128
NOTE = 16
CUTS = (0, 512, 896, 1024)
DIGIT = 128
DEAD = DIGIT**3 - 1
NONE = -1e30
AXES = ("blk", "grp")
SMEM = pl.BlockSpec(memory_space=pltpu.SMEM)
VMEM = pl.BlockSpec(memory_space=pltpu.VMEM)
HBM = pl.BlockSpec(memory_space=pltpu.HBM)


def passed_along(value, steps):
    count = lax.axis_size(AXES)
    leading, last = (max(0, -steps), min(count, count - steps))
    return lax.ppermute(value, AXES, [(source, source + steps) for source in range(leading, last)])


def shaped(shape, dtype):
    return jax.ShapeDtypeStruct(shape, dtype)


def unit_rows(raw):
    values = raw.astype(jnp.float32)
    scaling = lax.rsqrt(jnp.sum(values * values, axis=-1, keepdims=True) + 1e-06)
    return (values * scaling).astype(jnp.bfloat16)


def normalize(raw, units, rows):
    def step(index, carry):
        at = pl.ds(pl.multiple_of(index * LANES, LANES), LANES)
        units[at, :] = unit_rows(raw[at, :])
        return carry

    lax.fori_loop(0, rows // LANES, step, 0, unroll=2 if rows % (2 * LANES) == 0 else True)


def spread(keys_row):
    return jnp.broadcast_to(keys_row, (LANES, LANES)).T


def gathered(partial):
    return jnp.max(partial.T, axis=0, keepdims=True)


def shifted(found):
    return jnp.maximum(1.0 + found, 0.0)


def pair_tile(left_units, left_keys, right_units, right_keys):
    similarity = lax.dot_general(
        left_units, right_units, (((1,), (1,)), ((), ())), preferred_element_type=jnp.float32
    )
    rows, cols = similarity.shape
    left_best = None
    right_best = []
    for group in range(cols // LANES):
        part = similarity[:, group * LANES : (group + 1) * LANES]
        keys = right_keys[:, group * LANES : (group + 1) * LANES]
        for_left = jnp.where(keys < left_keys, part, NONE)
        left_best = for_left if left_best is None else jnp.maximum(left_best, for_left)
        for_right = jnp.where(left_keys < keys, part, NONE)
        right_best.append(jnp.max(for_right.reshape(rows // 8, 8, LANES), axis=0))
    return left_best, jnp.concatenate(right_best, axis=1)


def pair_strip(first, left_units, left_keys, left_acc, right_units, right_keys, right_acc, cols):
    rows = pl.ds(first, left_units.shape[0] - first)
    left_best, right_best = pair_tile(left_units[rows, :], left_keys[rows, :], right_units[cols, :], right_keys[:, cols])
    left_acc[rows, :] = jnp.maximum(left_acc[rows, :], left_best)
    right_acc[:, cols] = jnp.maximum(right_acc[:, cols], right_best)


def note_rows(keys, flags):
    row = lax.broadcasted_iota(jnp.int32, (NOTE, ROWS), 0)
    values = [keys % DIGIT, (keys // DIGIT) % DIGIT, keys // DIGIT**2] + flags
    note = jnp.zeros((NOTE, ROWS), jnp.int32)
    for index, value in enumerate(values):
        note = jnp.where(row == index, value, note)
    return note.astype(jnp.float32).astype(jnp.bfloat16)


def noted_keys(note):
    digits = note.astype(jnp.float32).astype(jnp.int32)
    return digits[0:1] + digits[1:2] * DIGIT + digits[2:3] * DIGIT**2


def piece_copies(index, raw, onward, back, sems):
    first, rows = CUTS[index], CUTS[index + 1] - CUTS[index]
    copies = [
        pltpu.make_async_copy(raw.at[block, pl.ds(first, rows)], piece.at[pl.ds(0, rows)], sems.at[side])
        for side, (block, piece) in enumerate(((HELD - 1, onward), (0, back)))
    ]
    for copy in copies:
        copy.start()
    return copies


def first_kernel(pairs, count, live, ranks, raw, onward, back, keys, flags, sems):
    copies = piece_copies(0, raw, onward, back, sems)
    position = lax.broadcasted_iota(jnp.int32, (1, ROWS), 1)
    for block in range(HELD):
        keys[block : block + 1, :] = jnp.where(position < live[block], ranks[block : block + 1, :], DEAD)

    def listed(u, v):
        found = jnp.int32(0)
        for slot in range(pairs.shape[2]):
            hit = (slot < count[0]) & (pairs[0, 0, slot] == u) & (pairs[0, 1, slot] == v)
            found = found | hit.astype(jnp.int32)
        return found

    ahead, near, far = listed(HELD + 1, HELD - 1), listed(HELD, HELD - 1), listed(HELD, HELD - 2)
    flags[0] = ahead * near
    flags[1] = ahead
    onward[pl.ds(CUTS[1], NOTE), :] = note_rows(keys[HELD - 1 : HELD, :], [])
    back[pl.ds(CUTS[1], NOTE), :] = note_rows(keys[0:1, :], [(1 - ahead) * near, far])
    for copy in copies:
        copy.wait()


def first_pieces(pairs, count, live, ranks, raw):
    piece = shaped((CUTS[1] + NOTE, DIM), jnp.bfloat16)
    pairs, live, ranks, raw = (pltpu.with_memory_space_constraint(value, pltpu.HBM) for value in (pairs, live, ranks, raw))
    return pl.pallas_call(
        first_kernel,
        out_shape=(piece, piece, shaped((HELD, ROWS), jnp.int32), shaped((2,), jnp.int32)),
        in_specs=[SMEM, SMEM, SMEM, VMEM, HBM],
        out_specs=(VMEM, VMEM, VMEM, SMEM),
        scratch_shapes=[pltpu.SemaphoreType.DMA((2,))],
        compiler_params=pltpu.CompilerParams(vmem_limit_bytes=6 << 20),
        cost_estimate=pl.CostEstimate(flops=0, bytes_accessed=8 * CUTS[1] * DIM, transcendentals=0),
    )(pairs, count, live, ranks, raw)


def later_kernel(index, flags, raw, after, onward, back, flags_again, sems):
    copies = piece_copies(index, raw, onward, back, sems)
    flags_again[0] = flags[0]
    flags_again[1] = flags[1]
    for copy in copies:
        copy.wait()


def later_pieces(index, flags, raw, after):
    rows = CUTS[index + 1] - CUTS[index]
    piece = shaped((rows, DIM), jnp.bfloat16)
    return pl.pallas_call(
        functools.partial(later_kernel, index),
        out_shape=(piece, piece, shaped((2,), jnp.int32)),
        in_specs=[SMEM, HBM, pl.BlockSpec(memory_space=pl.ANY)],
        out_specs=(VMEM, VMEM, SMEM),
        scratch_shapes=[pltpu.SemaphoreType.DMA((2,))],
        compiler_params=pltpu.CompilerParams(vmem_limit_bytes=4 << 20),
        cost_estimate=pl.CostEstimate(flops=0, bytes_accessed=8 * rows * DIM, transcendentals=0),
    )(flags, pltpu.with_memory_space_constraint(raw, pltpu.HBM), after)


def local_kernel(pairs, count, flags, raw, keys, units, best, spread_keys, left_acc, right_acc):
    for block in range(HELD):
        for group in range(ROWS // LANES):
            rows = pl.ds(group * LANES, LANES)
            spread_keys[block, rows, :] = spread(keys[block : block + 1, rows])
        normalize(raw.at[block], units.at[block], ROWS)
    left_acc[...] = jnp.full_like(left_acc, NONE)
    right_acc[...] = jnp.full_like(right_acc, NONE)

    def visit(slot, carry):
        left, right = pairs[0, 0, slot] - HELD, pairs[0, 1, slot] - HELD

        def strip(first, col):
            pair_strip(
                first, units.at[left], spread_keys.at[left], left_acc.at[left],
                units.at[right], keys.at[pl.ds(right, 1)], right_acc.at[right], pl.ds(col, COLS),
            )

        @pl.when(right == left)
        def _():
            for col in range(0, ROWS, COLS):
                strip(col, col)

        @pl.when((right >= 0) & (right != left))
        def _():
            for col in range(0, ROWS, COLS):
                strip(0, col)

        return carry

    lax.fori_loop(0, count[0], visit, 0)
    for block in range(HELD):
        for group in range(ROWS // LANES):
            rows = pl.ds(group * LANES, LANES)
            found = jnp.maximum(
                gathered(left_acc[block, rows, :]),
                jnp.max(right_acc[block, :, rows], axis=0, keepdims=True),
            )
            best[block : block + 1, rows] = shifted(found)


def local_pairs(pairs, count, flags, raw, keys):
    return pl.pallas_call(
        local_kernel,
        out_shape=(shaped((HELD, ROWS, DIM), jnp.bfloat16), shaped((HELD, ROWS), jnp.float32)),
        in_specs=[SMEM, SMEM, SMEM, VMEM, VMEM],
        out_specs=(VMEM, VMEM),
        scratch_shapes=[
            pltpu.VMEM((HELD, ROWS, LANES), jnp.int32),
            pltpu.VMEM((HELD, ROWS, LANES), jnp.float32),
            pltpu.VMEM((HELD, 8, ROWS), jnp.float32),
        ],
        compiler_params=pltpu.CompilerParams(vmem_limit_bytes=24 << 20),
        cost_estimate=pl.CostEstimate(flops=6 * 2 * ROWS * ROWS * DIM, bytes_accessed=4 * HELD * ROWS * DIM, transcendentals=0),
    )(pairs, count, flags, raw, keys)


def guest_pairs(flags, block_of, raw, rows, guest_keys, keys, units, right_acc, guest_units, spread_keys, left_acc):
    left_acc[...] = jnp.full_like(left_acc, NONE)
    some_live = jnp.min(guest_keys[:, :LANES].astype(jnp.float32)) < DEAD

    @pl.when(((flags[0] != 0) | (flags[1] != 0)) & some_live)
    def _():
        normalize(raw, guest_units, rows)
        for group in range(rows // LANES):
            at = pl.ds(group * LANES, LANES)
            spread_keys[at, :] = spread(guest_keys[:, group * LANES : (group + 1) * LANES])

        def visit(which, carry):
            block = block_of(which)

            @pl.when(flags[which] != 0)
            def _():
                for col in range(0, ROWS, COLS):
                    pair_strip(
                        0, guest_units, spread_keys, left_acc,
                        units.at[block], keys.at[pl.ds(block, 1)], right_acc.at[block], pl.ds(col, COLS),
                    )

            return carry

        lax.fori_loop(0, 2, visit, 0)


def finish_guests(left_acc, first, guest_earlier, guest_best):
    if first:
        guest_best[:, pl.ds(0, first)] = guest_earlier[...]
    for group in range(left_acc.shape[0] // LANES):
        found = gathered(left_acc[pl.ds(group * LANES, LANES), :])
        guest_best[:, pl.ds(first + group * LANES, LANES)] = shifted(found)


def finish_held(right_acc, best_before, best):
    for block in range(HELD):
        found = jnp.max(right_acc[block], axis=0, keepdims=True)
        best[block : block + 1, :] = jnp.maximum(best_before[block : block + 1, :], shifted(found))


def from_before(which):
    return which


def from_after(which):
    return HELD - 1 - which


def guest_scratch(rows):
    return [
        pltpu.VMEM((HELD, 8, ROWS), jnp.float32),
        pltpu.VMEM((rows, DIM), jnp.bfloat16),
        pltpu.VMEM((rows, LANES), jnp.int32),
        pltpu.VMEM((rows, LANES), jnp.float32),
    ]


def guest_cost(rows, blocks):
    return pl.CostEstimate(flops=2 * blocks * rows * ROWS * DIM, bytes_accessed=2 * (rows + HELD * ROWS) * DIM, transcendentals=0)


def both_first_kernel(
    flags, raw_before, raw_after, keys, units, best_before,
    guest_before, guest_after, best, keys_before, keys_after, flags_after, right_acc, *scratch,
):
    rows = CUTS[1]
    keys_before[...] = noted_keys(raw_before[pl.ds(rows, NOTE), :])
    note = raw_after[pl.ds(rows, NOTE), :]
    keys_after[...] = noted_keys(note)
    for which in range(2):
        flags_after[which] = (jnp.max(note[3 + which : 4 + which, :].astype(jnp.float32)) > 0.5).astype(jnp.int32)
    right_acc[...] = jnp.full_like(right_acc, NONE)
    left_acc = scratch[-1]
    guest_pairs(flags, from_before, raw_before, rows, keys_before[:, :rows], keys, units, right_acc, *scratch)
    finish_guests(left_acc, 0, None, guest_before)
    guest_pairs(flags_after, from_after, raw_after, rows, keys_after[:, :rows], keys, units, right_acc, *scratch)
    finish_guests(left_acc, 0, None, guest_after)
    finish_held(right_acc, best_before, best)


def both_first(flags, raw_before, raw_after, keys, units, best_before):
    row = shaped((1, ROWS), jnp.int32)
    guest = shaped((1, CUTS[1]), jnp.float32)
    return pl.pallas_call(
        both_first_kernel,
        out_shape=(guest, guest, shaped((HELD, ROWS), jnp.float32), row, row, shaped((2,), jnp.int32)),
        in_specs=[SMEM] + [VMEM] * 5,
        out_specs=(VMEM,) * 5 + (SMEM,),
        scratch_shapes=guest_scratch(CUTS[1]),
        compiler_params=pltpu.CompilerParams(vmem_limit_bytes=16 << 20),
        cost_estimate=guest_cost(CUTS[1], 3),
    )(flags, raw_before, raw_after, keys, units, best_before)


def both_next_kernel(
    flags, flags_after, raw_before, raw_after, keys_before, keys_after, keys, units, early_before, early_after, best_before,
    guest_before, guest_after, best, right_acc, *scratch,
):
    first, last = CUTS[1], CUTS[2]
    right_acc[...] = jnp.full_like(right_acc, NONE)
    left_acc = scratch[-1]
    guest_pairs(flags, from_before, raw_before, last - first, keys_before[:, first:last], keys, units, right_acc, *scratch)
    finish_guests(left_acc, first, early_before, guest_before)
    guest_pairs(flags_after, from_after, raw_after, last - first, keys_after[:, first:last], keys, units, right_acc, *scratch)
    finish_guests(left_acc, first, early_after, guest_after)
    finish_held(right_acc, best_before, best)


def both_next(flags, flags_after, raw_before, raw_after, keys_before, keys_after, keys, units, early_before, early_after, best_before):
    guest = shaped((1, CUTS[2]), jnp.float32)
    return pl.pallas_call(
        both_next_kernel,
        out_shape=(guest, guest, shaped((HELD, ROWS), jnp.float32)),
        in_specs=[SMEM, SMEM] + [VMEM] * 9,
        out_specs=(VMEM,) * 3,
        scratch_shapes=guest_scratch(CUTS[2] - CUTS[1]),
        compiler_params=pltpu.CompilerParams(vmem_limit_bytes=16 << 20),
        cost_estimate=guest_cost(CUTS[2] - CUTS[1], 3),
    )(flags, flags_after, raw_before, raw_after, keys_before, keys_after, keys, units, early_before, early_after, best_before)


def last_kernel(
    block_of, flags, raw, guest_keys, keys, units, guest_earlier, best_before, guest_best, best, right_acc, *scratch
):
    first, last = CUTS[2], CUTS[3]
    right_acc[...] = jnp.full_like(right_acc, NONE)
    guest_pairs(flags, block_of, raw, last - first, guest_keys[:, first:last], keys, units, right_acc, *scratch)
    finish_guests(scratch[-1], first, guest_earlier, guest_best)
    finish_held(right_acc, best_before, best)


def one_last(block_of, flags, raw, guest_keys, keys, units, guest_earlier, best_before):
    return pl.pallas_call(
        functools.partial(last_kernel, block_of),
        out_shape=(shaped((1, ROWS), jnp.float32), shaped((HELD, ROWS), jnp.float32)),
        in_specs=[SMEM] + [VMEM] * 6,
        out_specs=(VMEM, VMEM),
        scratch_shapes=guest_scratch(CUTS[3] - CUTS[2]),
        compiler_params=pltpu.CompilerParams(vmem_limit_bytes=12 << 20),
        cost_estimate=guest_cost(CUTS[3] - CUTS[2], 2),
    )(flags, raw, guest_keys, keys, units, guest_earlier, best_before)


def local(embeddings, ranks, block_rows, pair_list, pair_count):
    pairs = pair_list.transpose(0, 2, 1)
    on, back, keys, flags = first_pieces(pairs, pair_count, block_rows, ranks, embeddings)
    first_before, first_after = passed_along(on, 1), passed_along(back, -1)
    units, best = local_pairs(pairs, pair_count, flags, embeddings, keys)

    on, back, flags = later_pieces(1, flags, embeddings, best)
    next_before, next_after = passed_along(on, 1), passed_along(back, -1)
    guest_before, guest_after, best, keys_before, keys_after, flags_after = both_first(
        flags, first_before, first_after, keys, units, best
    )

    on, back, flags = later_pieces(2, flags, embeddings, best)
    last_before, last_after = passed_along(on, 1), passed_along(back, -1)
    guest_before, guest_after, best = both_next(
        flags, flags_after, next_before, next_after, keys_before, keys_after, keys, units, guest_before, guest_after, best
    )

    found, best = one_last(from_before, flags, last_before, keys_before, keys, units, guest_before, best)
    returned_back = passed_along(found, -1)
    found, best = one_last(from_after, flags_after, last_after, keys_after, keys, units, guest_after, best)
    returned_on = passed_along(found, 1)
    found = jnp.concatenate([returned_on, jnp.zeros_like(returned_on), returned_back], axis=0)
    return jnp.where(keys != DEAD, jnp.maximum(best, found), 0.0)


def solution(mesh):
    in_specs = (
        P(AXES, None, None),
        P(AXES, None),
        P(AXES),
        P(AXES, None, None),
        P(AXES),
    )
    return jax.shard_map(local, mesh=mesh, in_specs=in_specs, out_specs=P(AXES, None), check_vma=False)
```

```python
import functools

import jax
import jax.numpy as jnp
from jax import lax
from jax.experimental import pallas as pl
from jax.experimental.pallas import tpu as pltpu
from jax.sharding import PartitionSpec as P

ROWS = 1024
DIM = 1024
HELD = 3
COLS = 256
LANES = 128
NOTE = 16
CUTS = (0, 512, 896, 1024)
DIGIT = 128
DEAD = DIGIT**3 - 1
NONE = -1e30
AXES = ("blk", "grp")
SMEM = pl.BlockSpec(memory_space=pltpu.SMEM)
VMEM = pl.BlockSpec(memory_space=pltpu.VMEM)
HBM = pl.BlockSpec(memory_space=pltpu.HBM)


def exchanged(value, first):
    count = lax.axis_size(AXES)
    pairs = [(low, low + 1) for low in range(first, count - 1, 2)]
    return lax.ppermute(value, AXES, pairs + [(high, low) for low, high in pairs])


def odd_device():
    return lax.axis_index(AXES[-1]) % 2


def shaped(shape, dtype):
    return jax.ShapeDtypeStruct(shape, dtype)


def unit_rows(raw):
    values = raw.astype(jnp.float32)
    scaling = lax.rsqrt(jnp.sum(values * values, axis=-1, keepdims=True) + 1e-06)
    return (values * scaling).astype(jnp.bfloat16)


def normalize(raw, units, rows):
    def step(index, carry):
        at = pl.ds(pl.multiple_of(index * LANES, LANES), LANES)
        units[at, :] = unit_rows(raw[at, :])
        return carry

    lax.fori_loop(0, rows // LANES, step, 0, unroll=2 if rows % (2 * LANES) == 0 else True)


def spread(keys_row):
    return jnp.broadcast_to(keys_row, (LANES, LANES)).T


def gathered(partial):
    return jnp.max(partial.T, axis=0, keepdims=True)


def shifted(found):
    return jnp.maximum(1.0 + found, 0.0)


def pair_tile(left_units, left_keys, right_units, right_keys):
    similarity = lax.dot_general(
        left_units, right_units, (((1,), (1,)), ((), ())), preferred_element_type=jnp.float32
    )
    rows, cols = similarity.shape
    left_best = None
    right_best = []
    for group in range(cols // LANES):
        part = similarity[:, group * LANES : (group + 1) * LANES]
        keys = right_keys[:, group * LANES : (group + 1) * LANES]
        for_left = jnp.where(keys < left_keys, part, NONE)
        left_best = for_left if left_best is None else jnp.maximum(left_best, for_left)
        for_right = jnp.where(left_keys < keys, part, NONE)
        right_best.append(jnp.max(for_right.reshape(rows // 8, 8, LANES), axis=0))
    return left_best, jnp.concatenate(right_best, axis=1)


def pair_strip(first, left_units, left_keys, left_acc, right_units, right_keys, right_acc, cols):
    rows = pl.ds(first, left_units.shape[0] - first)
    left_best, right_best = pair_tile(left_units[rows, :], left_keys[rows, :], right_units[cols, :], right_keys[:, cols])
    left_acc[rows, :] = jnp.maximum(left_acc[rows, :], left_best)
    right_acc[:, cols] = jnp.maximum(right_acc[:, cols], right_best)


def note_rows(keys, flags):
    row = lax.broadcasted_iota(jnp.int32, (NOTE, ROWS), 0)
    values = [keys % DIGIT, (keys // DIGIT) % DIGIT, keys // DIGIT**2] + flags
    note = jnp.zeros((NOTE, ROWS), jnp.int32)
    for index, value in enumerate(values):
        note = jnp.where(row == index, value, note)
    return note.astype(jnp.float32).astype(jnp.bfloat16)


def noted_keys(note):
    digits = note.astype(jnp.float32).astype(jnp.int32)
    return digits[0:1] + digits[1:2] * DIGIT + digits[2:3] * DIGIT**2


def piece_copies(index, odd, raw, to_even, to_odd, sems):
    first, rows = CUTS[index], CUTS[index + 1] - CUTS[index]
    last_block = HELD - 1
    return [
        pltpu.make_async_copy(raw.at[block, pl.ds(first, rows)], piece.at[pl.ds(0, rows)], sems.at[index, side])
        for side, (block, piece) in enumerate(((last_block * (1 - odd), to_even), (last_block * odd, to_odd)))
    ]


def first_kernel(
    pairs_hbm, live_hbm, ranks_hbm, raw, even_on, odd_on, keys, flags,
    pairs, live, ranks, sems, small_sems,
):
    odd = odd_device()
    copies = piece_copies(0, odd, raw, even_on, odd_on, sems)
    small = [
        pltpu.make_async_copy(source, target, small_sems.at[index])
        for index, (source, target) in enumerate(((pairs_hbm, pairs), (live_hbm, live), (ranks_hbm, ranks)))
    ]
    for copy in small + copies:
        copy.start()
    for copy in small:
        copy.wait()
    position = lax.broadcasted_iota(jnp.int32, (1, ROWS), 1)
    for block in range(HELD):
        keys[block : block + 1, :] = jnp.where(position < live[block], ranks[block : block + 1, :], DEAD)

    def listed(u, v):
        found = jnp.int32(0)
        for slot in range(pairs.shape[2]):
            found = found | ((pairs[0, 0, slot] == u) & (pairs[0, 1, slot] == v)).astype(jnp.int32)
        return found

    ahead, near, far = listed(HELD + 1, HELD - 1), listed(HELD, HELD - 1), listed(HELD, HELD - 2)
    flags[0] = ahead * near
    flags[1] = ahead
    note_last = note_rows(keys[HELD - 1 : HELD, :], [])
    note_first = note_rows(keys[0:1, :], [(1 - ahead) * near, far])
    even_on[pl.ds(CUTS[1], NOTE), :] = jnp.where(odd == 1, note_first, note_last)
    odd_on[pl.ds(CUTS[1], NOTE), :] = jnp.where(odd == 1, note_last, note_first)
    for copy in copies:
        copy.wait()


def in_hbm(*values):
    return [pltpu.with_memory_space_constraint(value, pltpu.HBM) for value in values]


def first_pieces(pairs, live, ranks, raw):
    piece = shaped((CUTS[1] + NOTE, DIM), jnp.bfloat16)
    return pl.pallas_call(
        first_kernel,
        out_shape=(piece, piece, shaped((HELD, ROWS), jnp.int32), shaped((2,), jnp.int32)),
        in_specs=[HBM] * 4,
        out_specs=(VMEM,) * 3 + (SMEM,),
        scratch_shapes=[
            pltpu.SMEM(pairs.shape, jnp.int32),
            pltpu.SMEM(live.shape, jnp.int32),
            pltpu.VMEM(ranks.shape, jnp.int32),
            pltpu.SemaphoreType.DMA((2, 2)),
            pltpu.SemaphoreType.DMA((3,)),
        ],
        compiler_params=pltpu.CompilerParams(vmem_limit_bytes=6 << 20),
        cost_estimate=pl.CostEstimate(flops=0, bytes_accessed=8 * CUTS[1] * DIM, transcendentals=0),
    )(*in_hbm(pairs, live, ranks, raw))


def local_kernel(pairs, count, raw, keys, units, best, even_on, odd_on, spread_keys, left_acc, right_acc, sems):
    copies = piece_copies(1, odd_device(), raw, even_on, odd_on, sems)
    for copy in copies:
        copy.start()
    for block in range(HELD):
        for group in range(ROWS // LANES):
            rows = pl.ds(group * LANES, LANES)
            spread_keys[block, rows, :] = spread(keys[block : block + 1, rows])
        normalize(raw.at[block], units.at[block], ROWS)
    left_acc[...] = jnp.full_like(left_acc, NONE)
    right_acc[...] = jnp.full_like(right_acc, NONE)

    def visit(slot, carry):
        left, right = pairs[0, 0, slot] - HELD, pairs[0, 1, slot] - HELD

        def strip(first, col):
            pair_strip(
                first, units.at[left], spread_keys.at[left], left_acc.at[left],
                units.at[right], keys.at[pl.ds(right, 1)], right_acc.at[right], pl.ds(col, COLS),
            )

        @pl.when(right == left)
        def _():
            for col in range(0, ROWS, COLS):
                strip(col, col)

        @pl.when((right >= 0) & (right != left))
        def _():
            for col in range(0, ROWS, COLS):
                strip(0, col)

        return carry

    lax.fori_loop(0, count[0], visit, 0)
    for block in range(HELD):
        for group in range(ROWS // LANES):
            rows = pl.ds(group * LANES, LANES)
            found = jnp.maximum(
                gathered(left_acc[block, rows, :]),
                jnp.max(right_acc[block, :, rows], axis=0, keepdims=True),
            )
            best[block : block + 1, rows] = shifted(found)
    for copy in copies:
        copy.wait()


def local_pairs(pairs, count, raw, keys):
    piece = shaped((CUTS[2] - CUTS[1], DIM), jnp.bfloat16)
    return pl.pallas_call(
        local_kernel,
        out_shape=(shaped((HELD, ROWS, DIM), jnp.bfloat16), shaped((HELD, ROWS), jnp.float32), piece, piece),
        in_specs=[SMEM, SMEM, VMEM, VMEM],
        out_specs=(VMEM,) * 4,
        scratch_shapes=[
            pltpu.VMEM((HELD, ROWS, LANES), jnp.int32),
            pltpu.VMEM((HELD, ROWS, LANES), jnp.float32),
            pltpu.VMEM((HELD, 8, ROWS), jnp.float32),
            pltpu.SemaphoreType.DMA((3, 2)),
        ],
        compiler_params=pltpu.CompilerParams(vmem_limit_bytes=24 << 20),
        cost_estimate=pl.CostEstimate(flops=6 * 2 * ROWS * ROWS * DIM, bytes_accessed=4 * HELD * ROWS * DIM, transcendentals=0),
    )(pairs, count, raw, keys)


def last_kernel(raw, after, even_on, odd_on, sems):
    copies = piece_copies(2, odd_device(), raw, even_on, odd_on, sems)
    for copy in copies:
        copy.start()
    for copy in copies:
        copy.wait()


def last_pieces(raw, after):
    piece = shaped((CUTS[3] - CUTS[2], DIM), jnp.bfloat16)
    return pl.pallas_call(
        last_kernel,
        out_shape=(piece, piece),
        in_specs=[HBM, pl.BlockSpec(memory_space=pl.ANY)],
        out_specs=(VMEM, VMEM),
        scratch_shapes=[pltpu.SemaphoreType.DMA((3, 2))],
        compiler_params=pltpu.CompilerParams(vmem_limit_bytes=2 << 20),
        cost_estimate=pl.CostEstimate(flops=0, bytes_accessed=8 * (CUTS[3] - CUTS[2]) * DIM, transcendentals=0),
    )(*in_hbm(raw), after)


def guest_pairs(flags, after, raw, rows, guest_keys, keys, units, right_acc, guest_units, spread_keys, left_acc):
    cols = max(COLS, min(ROWS, COLS * ROWS // rows // COLS * COLS))
    left_acc[...] = jnp.full_like(left_acc, NONE)
    some_live = jnp.min(guest_keys[:, :LANES].astype(jnp.float32)) < DEAD

    @pl.when(((flags[0] != 0) | (flags[1] != 0)) & some_live)
    def _():
        normalize(raw, guest_units, rows)
        for group in range(rows // LANES):
            at = pl.ds(group * LANES, LANES)
            spread_keys[at, :] = spread(guest_keys[:, group * LANES : (group + 1) * LANES])

        def visit(which, carry):
            block = which + after * (HELD - 1 - 2 * which)

            @pl.when(flags[which] != 0)
            def _():
                for col in range(0, ROWS, cols):
                    pair_strip(
                        0, guest_units, spread_keys, left_acc,
                        units.at[block], keys.at[pl.ds(block, 1)], right_acc.at[block], pl.ds(col, cols),
                    )

            return carry

        lax.fori_loop(0, 2, visit, 0)


def finish_guests(left_acc, first, guest_earlier, guest_best):
    if first:
        guest_best[:, pl.ds(0, first)] = guest_earlier[...]
    for group in range(left_acc.shape[0] // LANES):
        found = gathered(left_acc[pl.ds(group * LANES, LANES), :])
        guest_best[:, pl.ds(first + group * LANES, LANES)] = shifted(found)


def finish_held(right_acc, best_before, best):
    for block in range(HELD):
        found = jnp.max(right_acc[block], axis=0, keepdims=True)
        best[block : block + 1, :] = jnp.maximum(best_before[block : block + 1, :], shifted(found))


def guest_scratch(rows):
    return [
        pltpu.VMEM((HELD, 8, ROWS), jnp.float32),
        pltpu.VMEM((rows, DIM), jnp.bfloat16),
        pltpu.VMEM((rows, LANES), jnp.int32),
        pltpu.VMEM((rows, LANES), jnp.float32),
    ]


def guest_cost(rows, blocks):
    return pl.CostEstimate(flops=2 * blocks * rows * ROWS * DIM, bytes_accessed=2 * (rows + HELD * ROWS) * DIM, transcendentals=0)


def first_guests_kernel(
    flags, even_raw, odd_raw, keys, units, best_before,
    even_guest, odd_guest, best, even_keys, odd_keys, even_flags, odd_flags, right_acc, *scratch,
):
    odd = odd_device()
    rows = CUTS[1]
    right_acc[...] = jnp.full_like(right_acc, NONE)
    sides = (
        (1 - odd, even_raw, even_keys, even_flags, even_guest),
        (odd, odd_raw, odd_keys, odd_flags, odd_guest),
    )
    for after, guest_raw, guest_keys, guest_flags, guest_best in sides:
        note = guest_raw[pl.ds(rows, NOTE), :]
        guest_keys[...] = noted_keys(note)
        for which in range(2):
            noted = (jnp.max(note[3 + which : 4 + which, :].astype(jnp.float32)) > 0.5).astype(jnp.int32)
            guest_flags[which] = jnp.where(after == 1, noted, flags[which])
        guest_pairs(guest_flags, after, guest_raw, rows, guest_keys[:, :rows], keys, units, right_acc, *scratch)
        finish_guests(scratch[-1], 0, None, guest_best)
    finish_held(right_acc, best_before, best)


def first_guests(flags, even_raw, odd_raw, keys, units, best_before):
    row = shaped((1, ROWS), jnp.int32)
    two = shaped((2,), jnp.int32)
    guest = shaped((1, CUTS[1]), jnp.float32)
    return pl.pallas_call(
        first_guests_kernel,
        out_shape=(guest, guest, shaped((HELD, ROWS), jnp.float32), row, row, two, two),
        in_specs=[SMEM] + [VMEM] * 5,
        out_specs=(VMEM,) * 5 + (SMEM,) * 2,
        scratch_shapes=guest_scratch(CUTS[1]),
        compiler_params=pltpu.CompilerParams(vmem_limit_bytes=16 << 20),
        cost_estimate=guest_cost(CUTS[1], 3),
    )(flags, even_raw, odd_raw, keys, units, best_before)


def next_guests_kernel(
    index, even_flags, odd_flags, even_raw, odd_raw, even_keys, odd_keys, keys, units, even_earlier, odd_earlier, best_before,
    even_guest, odd_guest, best, right_acc, *scratch,
):
    first, last = CUTS[index], CUTS[index + 1]
    odd = odd_device()
    right_acc[...] = jnp.full_like(right_acc, NONE)
    sides = (
        (1 - odd, even_raw, even_keys, even_flags, even_earlier, even_guest),
        (odd, odd_raw, odd_keys, odd_flags, odd_earlier, odd_guest),
    )
    for after, guest_raw, guest_keys, guest_flags, guest_earlier, guest_best in sides:
        guest_pairs(guest_flags, after, guest_raw, last - first, guest_keys[:, first:last], keys, units, right_acc, *scratch)
        finish_guests(scratch[-1], first, guest_earlier, guest_best)
    finish_held(right_acc, best_before, best)


def next_guests(index, even_flags, odd_flags, even_raw, odd_raw, even_keys, odd_keys, keys, units, *earlier):
    guest = shaped((1, CUTS[index + 1]), jnp.float32)
    rows = CUTS[index + 1] - CUTS[index]
    return pl.pallas_call(
        functools.partial(next_guests_kernel, index),
        out_shape=(guest, guest, shaped((HELD, ROWS), jnp.float32)),
        in_specs=[SMEM, SMEM] + [VMEM] * 9,
        out_specs=(VMEM,) * 3,
        scratch_shapes=guest_scratch(rows),
        compiler_params=pltpu.CompilerParams(vmem_limit_bytes=16 << 20),
        cost_estimate=guest_cost(rows, 3),
    )(even_flags, odd_flags, even_raw, odd_raw, even_keys, odd_keys, keys, units, *earlier)


def combined_kernel(keys, best_before, even_found, odd_found, best):
    odd = odd_device() == 1
    even, other = even_found[...], odd_found[...]
    found = (jnp.where(odd, even, other), jnp.zeros_like(even), jnp.where(odd, other, even))
    for block in range(HELD):
        rows = slice(block, block + 1)
        best[rows, :] = jnp.where(keys[rows, :] != DEAD, jnp.maximum(best_before[rows, :], found[block]), 0.0)


def combined(keys, best, even_found, odd_found):
    return pl.pallas_call(
        combined_kernel,
        out_shape=shaped((HELD, ROWS), jnp.float32),
        in_specs=[VMEM] * 4,
        out_specs=VMEM,
        compiler_params=pltpu.CompilerParams(vmem_limit_bytes=2 << 20),
        cost_estimate=pl.CostEstimate(flops=0, bytes_accessed=8 * HELD * ROWS, transcendentals=0),
    )(keys, best, even_found, odd_found)


def local(embeddings, ranks, block_rows, pair_list, pair_count):
    pairs = pair_list.transpose(0, 2, 1)
    even_on, odd_on, keys, flags = first_pieces(pairs, block_rows, ranks, embeddings)
    even_first, odd_first = exchanged(even_on, 0), exchanged(odd_on, 1)
    units, best, even_on, odd_on = local_pairs(pairs, pair_count, embeddings, keys)
    even_next, odd_next = exchanged(even_on, 0), exchanged(odd_on, 1)
    even_on, odd_on = last_pieces(embeddings, best)
    even_last, odd_last = exchanged(even_on, 0), exchanged(odd_on, 1)
    even_guest, odd_guest, best, even_keys, odd_keys, even_flags, odd_flags = first_guests(
        flags, even_first, odd_first, keys, units, best
    )
    known = (even_keys, odd_keys, keys, units)
    guests = next_guests(1, even_flags, odd_flags, even_next, odd_next, *known, even_guest, odd_guest, best)
    even_guest, odd_guest, best = next_guests(2, even_flags, odd_flags, even_last, odd_last, *known, *guests)
    even_found, odd_found = exchanged(even_guest, 0), exchanged(odd_guest, 1)
    return combined(keys, best, even_found, odd_found)


def solution(mesh):
    in_specs = (
        P(AXES, None, None),
        P(AXES, None),
        P(AXES),
        P(AXES, None, None),
        P(AXES),
    )
    return jax.shard_map(local, mesh=mesh, in_specs=in_specs, out_specs=P(AXES, None), check_vma=False)
```

```python
import functools

import jax
import jax.numpy as jnp
from jax import lax
from jax.experimental import pallas as pl
from jax.experimental.pallas import tpu as pltpu
from jax.sharding import PartitionSpec as P

ROWS = 1024
DIM = 1024
HELD = 3
COLS = 256
LANES = 128
NOTE = 16
CUTS = ((0, 640, 1024), (0, 640, 1024))
DIGIT = 128
DEAD = DIGIT**3 - 1
NONE = -1e30
AXES = ("blk", "grp")
SMEM = pl.BlockSpec(memory_space=pltpu.SMEM)
VMEM = pl.BlockSpec(memory_space=pltpu.VMEM)
HBM = pl.BlockSpec(memory_space=pltpu.HBM)


def exchanged(value, boundary):
    count = lax.axis_size(AXES)
    pairs = [(low, low + 1) for low in range(boundary, count - 1, 2)]
    return lax.ppermute(value, AXES, pairs + [(high, low) for low, high in pairs])


def odd_device():
    return lax.axis_index(AXES[-1]) % 2


def cut_rows(boundary, index):
    return CUTS[boundary][index + 1] - CUTS[boundary][index]


def shaped(shape, dtype):
    return jax.ShapeDtypeStruct(shape, dtype)


def unit_rows(raw):
    values = raw.astype(jnp.float32)
    scaling = lax.rsqrt(jnp.sum(values * values, axis=-1, keepdims=True) + 1e-06)
    return (values * scaling).astype(jnp.bfloat16)


def normalize(raw, units, rows):
    def step(index, carry):
        at = pl.ds(pl.multiple_of(index * LANES, LANES), LANES)
        units[at, :] = unit_rows(raw[at, :])
        return carry

    lax.fori_loop(0, rows // LANES, step, 0, unroll=2 if rows % (2 * LANES) == 0 else True)


def spread(keys_row):
    return jnp.broadcast_to(keys_row, (LANES, LANES)).T


def gathered(partial):
    return jnp.max(partial.T, axis=0, keepdims=True)


def shifted(found):
    return jnp.maximum(1.0 + found, 0.0)


def pair_tile(left_units, left_keys, right_units, right_keys):
    similarity = lax.dot_general(
        left_units, right_units, (((1,), (1,)), ((), ())), preferred_element_type=jnp.float32
    )
    rows, cols = similarity.shape
    left_best = None
    right_best = []
    for group in range(cols // LANES):
        part = similarity[:, group * LANES : (group + 1) * LANES]
        keys = right_keys[:, group * LANES : (group + 1) * LANES]
        for_left = jnp.where(keys < left_keys, part, NONE)
        left_best = for_left if left_best is None else jnp.maximum(left_best, for_left)
        for_right = jnp.where(left_keys < keys, part, NONE)
        right_best.append(jnp.max(for_right.reshape(rows // 8, 8, LANES), axis=0))
    return left_best, jnp.concatenate(right_best, axis=1)


def pair_strip(first, left_units, left_keys, left_acc, right_units, right_keys, right_acc, cols):
    rows = pl.ds(first, left_units.shape[0] - first)
    left_best, right_best = pair_tile(left_units[rows, :], left_keys[rows, :], right_units[cols, :], right_keys[:, cols])
    left_acc[rows, :] = jnp.maximum(left_acc[rows, :], left_best)
    right_acc[:, cols] = jnp.maximum(right_acc[:, cols], right_best)


def note_rows(keys, flags):
    row = lax.broadcasted_iota(jnp.int32, (NOTE, ROWS), 0)
    values = [keys % DIGIT, (keys // DIGIT) % DIGIT, keys // DIGIT**2] + flags
    note = jnp.zeros((NOTE, ROWS), jnp.int32)
    for index, value in enumerate(values):
        note = jnp.where(row == index, value, note)
    return note.astype(jnp.float32).astype(jnp.bfloat16)


def noted_keys(note):
    digits = note.astype(jnp.float32).astype(jnp.int32)
    return digits[0:1] + digits[1:2] * DIGIT + digits[2:3] * DIGIT**2


def piece_copies(items, raw, pieces, sems):
    odd, copies = odd_device(), []
    for number, ((boundary, index), piece) in enumerate(zip(items, pieces)):
        first, rows = CUTS[boundary][index], cut_rows(boundary, index)
        block = (HELD - 1) * (odd if boundary else 1 - odd)
        copies.append(pltpu.make_async_copy(raw.at[block, pl.ds(first, rows)], piece.at[pl.ds(0, rows)], sems.at[number]))
    return copies


def first_kernel(
    pairs_hbm, live_hbm, ranks_hbm, raw, even_on, odd_on, keys, flags,
    pairs, live, ranks, sems, small_sems,
):
    odd = odd_device()
    copies = piece_copies(((0, 0), (1, 0)), raw, (even_on, odd_on), sems)
    small = [
        pltpu.make_async_copy(source, target, small_sems.at[index])
        for index, (source, target) in enumerate(((pairs_hbm, pairs), (live_hbm, live), (ranks_hbm, ranks)))
    ]
    for copy in small + copies:
        copy.start()
    for copy in small:
        copy.wait()
    position = lax.broadcasted_iota(jnp.int32, (1, ROWS), 1)
    for block in range(HELD):
        keys[block : block + 1, :] = jnp.where(position < live[block], ranks[block : block + 1, :], DEAD)

    def listed(u, v):
        found = jnp.int32(0)
        for slot in range(pairs.shape[2]):
            found = found | ((pairs[0, 0, slot] == u) & (pairs[0, 1, slot] == v)).astype(jnp.int32)
        return found

    ahead, near, far = listed(HELD + 1, HELD - 1), listed(HELD, HELD - 1), listed(HELD, HELD - 2)
    flags[0] = ahead * near
    flags[1] = ahead
    note_last = note_rows(keys[HELD - 1 : HELD, :], [])
    note_first = note_rows(keys[0:1, :], [(1 - ahead) * near, far])
    even_on[pl.ds(cut_rows(0, 0), NOTE), :] = jnp.where(odd == 1, note_first, note_last)
    odd_on[pl.ds(cut_rows(1, 0), NOTE), :] = jnp.where(odd == 1, note_last, note_first)
    for copy in copies:
        copy.wait()


def in_hbm(*values):
    return [pltpu.with_memory_space_constraint(value, pltpu.HBM) for value in values]


def first_pieces(pairs, live, ranks, raw):
    even, odd = (shaped((cut_rows(boundary, 0) + NOTE, DIM), jnp.bfloat16) for boundary in range(2))
    return pl.pallas_call(
        first_kernel,
        out_shape=(even, odd, shaped((HELD, ROWS), jnp.int32), shaped((2,), jnp.int32)),
        in_specs=[HBM] * 4,
        out_specs=(VMEM,) * 3 + (SMEM,),
        scratch_shapes=[
            pltpu.SMEM(pairs.shape, jnp.int32),
            pltpu.SMEM(live.shape, jnp.int32),
            pltpu.VMEM(ranks.shape, jnp.int32),
            pltpu.SemaphoreType.DMA((2,)),
            pltpu.SemaphoreType.DMA((3,)),
        ],
        compiler_params=pltpu.CompilerParams(vmem_limit_bytes=6 << 20),
        cost_estimate=pl.CostEstimate(flops=0, bytes_accessed=4 * ROWS * DIM, transcendentals=0),
    )(*in_hbm(pairs, live, ranks, raw))


def local_kernel(pairs, count, raw, keys, units, best, even_on, odd_on, spread_keys, left_acc, right_acc, sems):
    copies = piece_copies(((0, 1), (1, 1)), raw, (even_on, odd_on), sems)
    for copy in copies:
        copy.start()
    for block in range(HELD):
        for group in range(ROWS // LANES):
            rows = pl.ds(group * LANES, LANES)
            spread_keys[block, rows, :] = spread(keys[block : block + 1, rows])
        normalize(raw.at[block], units.at[block], ROWS)
    left_acc[...] = jnp.full_like(left_acc, NONE)
    right_acc[...] = jnp.full_like(right_acc, NONE)

    def visit(slot, carry):
        left, right = pairs[0, 0, slot] - HELD, pairs[0, 1, slot] - HELD

        def strip(first, col):
            pair_strip(
                first, units.at[left], spread_keys.at[left], left_acc.at[left],
                units.at[right], keys.at[pl.ds(right, 1)], right_acc.at[right], pl.ds(col, COLS),
            )

        @pl.when(right == left)
        def _():
            for col in range(0, ROWS, COLS):
                strip(col, col)

        @pl.when((right >= 0) & (right != left))
        def _():
            for col in range(0, ROWS, COLS):
                strip(0, col)

        return carry

    lax.fori_loop(0, count[0], visit, 0)
    for block in range(HELD):
        for group in range(ROWS // LANES):
            rows = pl.ds(group * LANES, LANES)
            found = jnp.maximum(
                gathered(left_acc[block, rows, :]),
                jnp.max(right_acc[block, :, rows], axis=0, keepdims=True),
            )
            best[block : block + 1, rows] = shifted(found)
    for copy in copies:
        copy.wait()


def local_pairs(pairs, count, raw, keys):
    even, odd = (shaped((cut_rows(boundary, 1), DIM), jnp.bfloat16) for boundary in range(2))
    return pl.pallas_call(
        local_kernel,
        out_shape=(shaped((HELD, ROWS, DIM), jnp.bfloat16), shaped((HELD, ROWS), jnp.float32), even, odd),
        in_specs=[SMEM, SMEM, VMEM, VMEM],
        out_specs=(VMEM,) * 4,
        scratch_shapes=[
            pltpu.VMEM((HELD, ROWS, LANES), jnp.int32),
            pltpu.VMEM((HELD, ROWS, LANES), jnp.float32),
            pltpu.VMEM((HELD, 8, ROWS), jnp.float32),
            pltpu.SemaphoreType.DMA((2,)),
        ],
        compiler_params=pltpu.CompilerParams(vmem_limit_bytes=24 << 20),
        cost_estimate=pl.CostEstimate(flops=2 * ROWS * ROWS * DIM, bytes_accessed=4 * HELD * ROWS * DIM, transcendentals=0),
    )(pairs, count, raw, keys)


def guest_pairs(flags, after, raw, rows, guest_keys, keys, units, right_acc, guest_units, spread_keys, left_acc):
    cols = max(COLS, min(ROWS, COLS * ROWS // rows // COLS * COLS))
    left_acc[...] = jnp.full_like(left_acc, NONE)
    some_live = jnp.min(guest_keys[:, :LANES].astype(jnp.float32)) < DEAD

    @pl.when(((flags[0] != 0) | (flags[1] != 0)) & some_live)
    def _():
        normalize(raw, guest_units, rows)
        for group in range(rows // LANES):
            at = pl.ds(group * LANES, LANES)
            spread_keys[at, :] = spread(guest_keys[:, group * LANES : (group + 1) * LANES])

        def visit(which, carry):
            block = which + after * (HELD - 1 - 2 * which)

            @pl.when(flags[which] != 0)
            def _():
                for col in range(0, ROWS, cols):
                    pair_strip(
                        0, guest_units, spread_keys, left_acc,
                        units.at[block], keys.at[pl.ds(block, 1)], right_acc.at[block], pl.ds(col, cols),
                    )

            return carry

        lax.fori_loop(0, 2, visit, 0)


def finish_guests(left_acc, first, guest_earlier, guest_best):
    if first:
        guest_best[:, pl.ds(0, first)] = guest_earlier[...]
    for group in range(left_acc.shape[0] // LANES):
        found = gathered(left_acc[pl.ds(group * LANES, LANES), :])
        guest_best[:, pl.ds(first + group * LANES, LANES)] = shifted(found)


def finish_held(right_acc, best_before, best):
    for block in range(HELD):
        found = jnp.max(right_acc[block], axis=0, keepdims=True)
        best[block : block + 1, :] = jnp.maximum(best_before[block : block + 1, :], shifted(found))


def guest_scratch(rows):
    return [
        pltpu.VMEM((HELD, 8, ROWS), jnp.float32),
        pltpu.VMEM((rows, DIM), jnp.bfloat16),
        pltpu.VMEM((rows, LANES), jnp.int32),
        pltpu.VMEM((rows, LANES), jnp.float32),
    ]


def guest_cost(rows):
    return pl.CostEstimate(flops=2 * rows * ROWS * DIM, bytes_accessed=2 * (rows + HELD * ROWS) * DIM, transcendentals=0)


def first_guests_kernel(
    boundary, flags, raw, keys, units, best_before, guest_best, best, guest_keys, guest_flags, right_acc, *scratch
):
    rows = cut_rows(boundary, 0)
    after = odd_device() if boundary else 1 - odd_device()
    right_acc[...] = jnp.full_like(right_acc, NONE)
    note = raw[pl.ds(rows, NOTE), :]
    guest_keys[...] = noted_keys(note)
    for which in range(2):
        noted = (jnp.max(note[3 + which : 4 + which, :].astype(jnp.float32)) > 0.5).astype(jnp.int32)
        guest_flags[which] = jnp.where(after == 1, noted, flags[which])
    guest_pairs(guest_flags, after, raw, rows, guest_keys[:, :rows], keys, units, right_acc, *scratch)
    finish_guests(scratch[-1], 0, None, guest_best)
    finish_held(right_acc, best_before, best)


def first_guests(boundary, flags, raw, keys, units, best_before):
    rows = cut_rows(boundary, 0)
    return pl.pallas_call(
        functools.partial(first_guests_kernel, boundary),
        out_shape=(
            shaped((1, rows), jnp.float32),
            shaped((HELD, ROWS), jnp.float32),
            shaped((1, ROWS), jnp.int32),
            shaped((2,), jnp.int32),
        ),
        in_specs=[SMEM] + [VMEM] * 4,
        out_specs=(VMEM, VMEM, VMEM, SMEM),
        scratch_shapes=guest_scratch(rows),
        compiler_params=pltpu.CompilerParams(vmem_limit_bytes=16 << 20),
        cost_estimate=guest_cost(rows),
    )(flags, raw, keys, units, best_before)


def next_guests_kernel(
    boundary, index, flags, raw, guest_keys, guest_earlier, keys, units, best_before, guest_best, best, right_acc, *scratch
):
    first, rows = CUTS[boundary][index], cut_rows(boundary, index)
    after = odd_device() if boundary else 1 - odd_device()
    right_acc[...] = jnp.full_like(right_acc, NONE)
    guest_pairs(flags, after, raw, rows, guest_keys[:, first : first + rows], keys, units, right_acc, *scratch)
    finish_guests(scratch[-1], first, guest_earlier, guest_best)
    finish_held(right_acc, best_before, best)


def next_guests(boundary, index, flags, *rest):
    rows = cut_rows(boundary, index)
    return pl.pallas_call(
        functools.partial(next_guests_kernel, boundary, index),
        out_shape=(shaped((1, CUTS[boundary][index + 1]), jnp.float32), shaped((HELD, ROWS), jnp.float32)),
        in_specs=[SMEM] + [VMEM] * len(rest),
        out_specs=(VMEM, VMEM),
        scratch_shapes=guest_scratch(rows),
        compiler_params=pltpu.CompilerParams(vmem_limit_bytes=16 << 20),
        cost_estimate=guest_cost(rows),
    )(flags, *rest)


def combined_kernel(keys, best_before, even_found, odd_found, best):
    odd = odd_device() == 1
    even, other = even_found[...], odd_found[...]
    found = (jnp.where(odd, even, other), jnp.zeros_like(even), jnp.where(odd, other, even))
    for block in range(HELD):
        rows = slice(block, block + 1)
        best[rows, :] = jnp.where(keys[rows, :] != DEAD, jnp.maximum(best_before[rows, :], found[block]), 0.0)


def combined(keys, best, even_found, odd_found):
    return pl.pallas_call(
        combined_kernel,
        out_shape=shaped((HELD, ROWS), jnp.float32),
        in_specs=[VMEM] * 4,
        out_specs=VMEM,
        compiler_params=pltpu.CompilerParams(vmem_limit_bytes=2 << 20),
        cost_estimate=pl.CostEstimate(flops=0, bytes_accessed=8 * HELD * ROWS, transcendentals=0),
    )(keys, best, even_found, odd_found)


def local(embeddings, ranks, block_rows, pair_list, pair_count):
    pairs = pair_list.transpose(0, 2, 1)
    even_on, odd_on, keys, flags = first_pieces(pairs, block_rows, ranks, embeddings)
    even_first, odd_first = exchanged(even_on, 0), exchanged(odd_on, 1)
    units, best, even_on, odd_on = local_pairs(pairs, pair_count, embeddings, keys)
    even_last, odd_last = exchanged(even_on, 0), exchanged(odd_on, 1)
    even_guest, best, even_keys, even_flags = first_guests(0, flags, even_first, keys, units, best)
    odd_guest, best, odd_keys, odd_flags = first_guests(1, flags, odd_first, keys, units, best)
    even_guest, best = next_guests(0, 1, even_flags, even_last, even_keys, even_guest, keys, units, best)
    even_found = exchanged(even_guest, 0)
    odd_guest, best = next_guests(1, 1, odd_flags, odd_last, odd_keys, odd_guest, keys, units, best)
    odd_found = exchanged(odd_guest, 1)
    return combined(keys, best, even_found, odd_found)


def solution(mesh):
    in_specs = (
        P(AXES, None, None),
        P(AXES, None),
        P(AXES),
        P(AXES, None, None),
        P(AXES),
    )
    return jax.shard_map(local, mesh=mesh, in_specs=in_specs, out_specs=P(AXES, None), check_vma=False)
```

```python
import functools

import jax
import jax.numpy as jnp
from jax import lax
from jax.experimental import pallas as pl
from jax.experimental.pallas import tpu as pltpu
from jax.sharding import PartitionSpec as P

ROWS = 1024
DIM = 1024
HELD = 3
COLS = 256
LANES = 128
NOTE = 16
CUTS = ((0, 640, 1024), (0, 640, 1024))
DIGIT = 128
DEAD = DIGIT**3 - 1
NONE = -1e30
AXES = ("blk", "grp")
SMEM = pl.BlockSpec(memory_space=pltpu.SMEM)
VMEM = pl.BlockSpec(memory_space=pltpu.VMEM)
HBM = pl.BlockSpec(memory_space=pltpu.HBM)


def exchanged(value, boundary):
    count = lax.axis_size(AXES)
    pairs = [(low, low + 1) for low in range(boundary, count - 1, 2)]
    return lax.ppermute(value, AXES, pairs + [(high, low) for low, high in pairs])


def odd_device():
    return lax.axis_index(AXES[-1]) % 2


def odd_after(boundary):
    return odd_device() if boundary else 1 - odd_device()


def cut_rows(boundary, index):
    return CUTS[boundary][index + 1] - CUTS[boundary][index]


def shaped(shape, dtype):
    return jax.ShapeDtypeStruct(shape, dtype)


def unit_rows(raw):
    values = raw.astype(jnp.float32)
    scaling = lax.rsqrt(jnp.sum(values * values, axis=-1, keepdims=True) + 1e-06)
    return (values * scaling).astype(jnp.bfloat16)


def normalize(raw, units, rows):
    def step(index, carry):
        at = pl.ds(pl.multiple_of(index * LANES, LANES), LANES)
        units[at, :] = unit_rows(raw[at, :])
        return carry

    lax.fori_loop(0, rows // LANES, step, 0, unroll=2 if rows % (2 * LANES) == 0 else True)


def spread(keys_row):
    return jnp.broadcast_to(keys_row, (LANES, LANES)).T


def gathered(partial):
    return jnp.max(partial.T, axis=0, keepdims=True)


def shifted(found):
    return jnp.maximum(1.0 + found, 0.0)


def pair_tile(left_units, left_keys, right_units, right_keys):
    similarity = lax.dot_general(
        left_units, right_units, (((1,), (1,)), ((), ())), preferred_element_type=jnp.float32
    )
    rows, cols = similarity.shape
    left_best = None
    right_best = []
    for group in range(cols // LANES):
        part = similarity[:, group * LANES : (group + 1) * LANES]
        keys = right_keys[:, group * LANES : (group + 1) * LANES]
        for_left = jnp.where(keys < left_keys, part, NONE)
        left_best = for_left if left_best is None else jnp.maximum(left_best, for_left)
        for_right = jnp.where(left_keys < keys, part, NONE)
        right_best.append(jnp.max(for_right.reshape(rows // 8, 8, LANES), axis=0))
    return left_best, jnp.concatenate(right_best, axis=1)


def pair_strip(first, left_units, left_keys, left_acc, right_units, right_keys, right_acc, cols):
    rows = pl.ds(first, left_units.shape[0] - first)
    left_best, right_best = pair_tile(left_units[rows, :], left_keys[rows, :], right_units[cols, :], right_keys[:, cols])
    left_acc[rows, :] = jnp.maximum(left_acc[rows, :], left_best)
    right_acc[:, cols] = jnp.maximum(right_acc[:, cols], right_best)


def note_rows(keys, flags):
    row = lax.broadcasted_iota(jnp.int32, (NOTE, ROWS), 0)
    values = [keys % DIGIT, (keys // DIGIT) % DIGIT, keys // DIGIT**2] + flags
    note = jnp.zeros((NOTE, ROWS), jnp.int32)
    for index, value in enumerate(values):
        note = jnp.where(row == index, value, note)
    return note.astype(jnp.float32).astype(jnp.bfloat16)


def noted_keys(note):
    digits = note.astype(jnp.float32).astype(jnp.int32)
    return digits[0:1] + digits[1:2] * DIGIT + digits[2:3] * DIGIT**2


def piece_copies(items, raw, pieces, sems):
    odd, copies = odd_device(), []
    for number, ((boundary, index), piece) in enumerate(zip(items, pieces)):
        first, rows = CUTS[boundary][index], cut_rows(boundary, index)
        block = (HELD - 1) * (odd if boundary else 1 - odd)
        copies.append(pltpu.make_async_copy(raw.at[block, pl.ds(first, rows)], piece.at[pl.ds(0, rows)], sems.at[number]))
    return copies


def boundary_flags(pairs):
    def listed(u, v):
        found = jnp.int32(0)
        for slot in range(pairs.shape[2]):
            found = found | ((pairs[0, 0, slot] == u) & (pairs[0, 1, slot] == v)).astype(jnp.int32)
        return found

    ahead, near, far = listed(HELD + 1, HELD - 1), listed(HELD, HELD - 1), listed(HELD, HELD - 2)
    here, there = ahead * near, (1 - ahead) * near
    return [here, ahead, there], [there, far, here]


def first_kernel(
    pairs_hbm, live_hbm, ranks_hbm, raw, even_on, odd_on, keys, pairs, live, ranks, sems, small_sems
):
    odd = odd_device()
    copies = piece_copies(((0, 0), (1, 0)), raw, (even_on, odd_on), sems)
    small = [
        pltpu.make_async_copy(source, target, small_sems.at[index])
        for index, (source, target) in enumerate(((pairs_hbm, pairs), (live_hbm, live), (ranks_hbm, ranks)))
    ]
    for copy in small + copies:
        copy.start()
    for copy in small:
        copy.wait()
    position = lax.broadcasted_iota(jnp.int32, (1, ROWS), 1)
    for block in range(HELD):
        keys[block : block + 1, :] = jnp.where(position < live[block], ranks[block : block + 1, :], DEAD)

    left_flags, right_flags = boundary_flags(pairs)
    note_last = note_rows(keys[HELD - 1 : HELD, :], [])
    note_first = note_rows(keys[0:1, :], right_flags)
    even_on[pl.ds(cut_rows(0, 0), NOTE), :] = jnp.where(odd == 1, note_first, note_last)
    odd_on[pl.ds(cut_rows(1, 0), NOTE), :] = jnp.where(odd == 1, note_last, note_first)
    for copy in copies:
        copy.wait()


def in_hbm(*values):
    return [pltpu.with_memory_space_constraint(value, pltpu.HBM) for value in values]


def first_pieces(pairs, live, ranks, raw):
    even, odd = (shaped((cut_rows(boundary, 0) + NOTE, DIM), jnp.bfloat16) for boundary in range(2))
    return pl.pallas_call(
        first_kernel,
        out_shape=(even, odd, shaped((HELD, ROWS), jnp.int32)),
        in_specs=[HBM] * 4,
        out_specs=(VMEM,) * 3,
        scratch_shapes=[
            pltpu.SMEM(pairs.shape, jnp.int32),
            pltpu.SMEM(live.shape, jnp.int32),
            pltpu.VMEM(ranks.shape, jnp.int32),
            pltpu.SemaphoreType.DMA((2,)),
            pltpu.SemaphoreType.DMA((3,)),
        ],
        compiler_params=pltpu.CompilerParams(vmem_limit_bytes=6 << 20),
        cost_estimate=pl.CostEstimate(flops=0, bytes_accessed=4 * ROWS * DIM, transcendentals=0),
    )(*in_hbm(pairs, live, ranks, raw))


def local_kernel(pairs, count, raw, keys, units, best, even_on, odd_on, flags, spread_keys, left_acc, right_acc, sems):
    copies = piece_copies(((0, 1), (1, 1)), raw, (even_on, odd_on), sems)
    for copy in copies:
        copy.start()
    for index, flag in enumerate(boundary_flags(pairs)[0]):
        flags[index] = flag
    for block in range(HELD):
        for group in range(ROWS // LANES):
            rows = pl.ds(group * LANES, LANES)
            spread_keys[block, rows, :] = spread(keys[block : block + 1, rows])
        normalize(raw.at[block], units.at[block], ROWS)
    left_acc[...] = jnp.full_like(left_acc, NONE)
    right_acc[...] = jnp.full_like(right_acc, NONE)

    def visit(slot, carry):
        left, right = pairs[0, 0, slot] - HELD, pairs[0, 1, slot] - HELD

        def strip(first, col):
            pair_strip(
                first, units.at[left], spread_keys.at[left], left_acc.at[left],
                units.at[right], keys.at[pl.ds(right, 1)], right_acc.at[right], pl.ds(col, COLS),
            )

        @pl.when(right == left)
        def _():
            for col in range(0, ROWS, COLS):
                strip(col, col)

        @pl.when((right >= 0) & (right != left))
        def _():
            for col in range(0, ROWS, COLS):
                strip(0, col)

        return carry

    lax.fori_loop(0, count[0], visit, 0)
    for block in range(HELD):
        for group in range(ROWS // LANES):
            rows = pl.ds(group * LANES, LANES)
            found = jnp.maximum(
                gathered(left_acc[block, rows, :]),
                jnp.max(right_acc[block, :, rows], axis=0, keepdims=True),
            )
            best[block : block + 1, rows] = shifted(found)
    for copy in copies:
        copy.wait()


def local_pairs(pairs, count, raw, keys):
    even, odd = (shaped((cut_rows(boundary, 1), DIM), jnp.bfloat16) for boundary in range(2))
    return pl.pallas_call(
        local_kernel,
        out_shape=(
            shaped((HELD, ROWS, DIM), jnp.bfloat16),
            shaped((HELD, ROWS), jnp.float32),
            even,
            odd,
            shaped((3,), jnp.int32),
        ),
        in_specs=[SMEM, SMEM, VMEM, VMEM],
        out_specs=(VMEM,) * 4 + (SMEM,),
        scratch_shapes=[
            pltpu.VMEM((HELD, ROWS, LANES), jnp.int32),
            pltpu.VMEM((HELD, ROWS, LANES), jnp.float32),
            pltpu.VMEM((HELD, 8, ROWS), jnp.float32),
            pltpu.SemaphoreType.DMA((2,)),
        ],
        compiler_params=pltpu.CompilerParams(vmem_limit_bytes=24 << 20),
        cost_estimate=pl.CostEstimate(flops=2 * ROWS * ROWS * DIM, bytes_accessed=4 * HELD * ROWS * DIM, transcendentals=0),
    )(pairs, count, raw, keys)


def guest_pairs(boundary, index, flags, raw, guest_keys, keys, units, right_acc, guest_units, spread_keys, left_acc):
    first, rows = CUTS[boundary][index], cut_rows(boundary, index)
    guest_keys = guest_keys[:, first : first + rows]
    beside = (HELD - 1) * (odd_after(boundary))
    cols = max(COLS, COLS * ROWS // rows // COLS * COLS)
    left_acc[...] = jnp.full_like(left_acc, NONE)
    some_live = jnp.min(guest_keys[:, :LANES].astype(jnp.float32)) < DEAD
    takes_beside = flags[0] if index == 0 else jnp.int32(0)

    def meet(block, low, high, width):
        for col in range(low, high, width):
            pair_strip(
                0, guest_units, spread_keys, left_acc,
                units.at[block], keys.at[pl.ds(block, 1)], right_acc.at[block], pl.ds(col, width),
            )

    @pl.when(((takes_beside != 0) | (flags[1] != 0) | (flags[2] != 0)) & some_live)
    def _():
        normalize(raw, guest_units, rows)
        for group in range(rows // LANES):
            at = pl.ds(group * LANES, LANES)
            spread_keys[at, :] = spread(guest_keys[:, group * LANES : (group + 1) * LANES])

        def visit(which, carry):
            @pl.when(flags[which] != 0)
            def _():
                meet(jnp.where(which == 0, beside, 1), 0, ROWS, cols)

            return carry

        lax.fori_loop(0 if index == 0 else 1, 2, visit, 0)

        @pl.when(flags[2] != 0)
        def _():
            low = CUTS[boundary][-2]
            meet(beside, low, ROWS, ROWS - low)


def finish_guests(left_acc, first, guest_earlier, guest_best):
    if first:
        guest_best[:, pl.ds(0, first)] = guest_earlier[...]
    for group in range(left_acc.shape[0] // LANES):
        found = gathered(left_acc[pl.ds(group * LANES, LANES), :])
        guest_best[:, pl.ds(first + group * LANES, LANES)] = shifted(found)


def finish_held(right_acc, best_before, best):
    for block in range(HELD):
        found = jnp.max(right_acc[block], axis=0, keepdims=True)
        best[block : block + 1, :] = jnp.maximum(best_before[block : block + 1, :], shifted(found))


def guest_scratch(rows):
    return [
        pltpu.VMEM((HELD, 8, ROWS), jnp.float32),
        pltpu.VMEM((rows, DIM), jnp.bfloat16),
        pltpu.VMEM((rows, LANES), jnp.int32),
        pltpu.VMEM((rows, LANES), jnp.float32),
    ]


def guest_cost(rows):
    return pl.CostEstimate(flops=2 * rows * ROWS * DIM, bytes_accessed=2 * (rows + HELD * ROWS) * DIM, transcendentals=0)


def first_guests_kernel(
    boundary, flags, raw, keys, units, best_before, guest_best, best, guest_keys, guest_flags, right_acc, *scratch
):
    rows = cut_rows(boundary, 0)
    after = odd_after(boundary)
    right_acc[...] = jnp.full_like(right_acc, NONE)
    note = raw[pl.ds(rows, NOTE), :]
    guest_keys[...] = noted_keys(note)
    for which in range(3):
        noted = (jnp.max(note[3 + which : 4 + which, :].astype(jnp.float32)) > 0.5).astype(jnp.int32)
        guest_flags[which] = jnp.where(after == 1, noted, flags[which])
    guest_pairs(boundary, 0, guest_flags, raw, guest_keys, keys, units, right_acc, *scratch)
    finish_guests(scratch[-1], 0, None, guest_best)
    finish_held(right_acc, best_before, best)


def first_guests(boundary, flags, raw, keys, units, best_before):
    rows = cut_rows(boundary, 0)
    return pl.pallas_call(
        functools.partial(first_guests_kernel, boundary),
        out_shape=(
            shaped((1, rows), jnp.float32),
            shaped((HELD, ROWS), jnp.float32),
            shaped((1, ROWS), jnp.int32),
            shaped((3,), jnp.int32),
        ),
        in_specs=[SMEM] + [VMEM] * 4,
        out_specs=(VMEM, VMEM, VMEM, SMEM),
        scratch_shapes=guest_scratch(rows),
        compiler_params=pltpu.CompilerParams(vmem_limit_bytes=16 << 20),
        cost_estimate=guest_cost(rows),
    )(flags, raw, keys, units, best_before)


def next_guests_kernel(
    boundary, index, flags, raw, guest_keys, guest_earlier, keys, units, best_before, guest_best, best, right_acc, *scratch
):
    right_acc[...] = jnp.full_like(right_acc, NONE)
    guest_pairs(boundary, index, flags, raw, guest_keys, keys, units, right_acc, *scratch)
    finish_guests(scratch[-1], CUTS[boundary][index], guest_earlier, guest_best)
    finish_held(right_acc, best_before, best)


def next_guests(boundary, index, flags, *rest):
    rows = cut_rows(boundary, index)
    return pl.pallas_call(
        functools.partial(next_guests_kernel, boundary, index),
        out_shape=(shaped((1, CUTS[boundary][index + 1]), jnp.float32), shaped((HELD, ROWS), jnp.float32)),
        in_specs=[SMEM] + [VMEM] * len(rest),
        out_specs=(VMEM, VMEM),
        scratch_shapes=guest_scratch(rows),
        compiler_params=pltpu.CompilerParams(vmem_limit_bytes=16 << 20),
        cost_estimate=guest_cost(rows),
    )(flags, *rest)


def combined_kernel(keys, best_before, even_found, odd_found, best):
    odd = odd_device() == 1
    even, other = even_found[...], odd_found[...]
    found = (jnp.where(odd, even, other), jnp.zeros_like(even), jnp.where(odd, other, even))
    for block in range(HELD):
        rows = slice(block, block + 1)
        best[rows, :] = jnp.where(keys[rows, :] != DEAD, jnp.maximum(best_before[rows, :], found[block]), 0.0)


def combined(keys, best, even_found, odd_found):
    return pl.pallas_call(
        combined_kernel,
        out_shape=shaped((HELD, ROWS), jnp.float32),
        in_specs=[VMEM] * 4,
        out_specs=VMEM,
        compiler_params=pltpu.CompilerParams(vmem_limit_bytes=2 << 20),
        cost_estimate=pl.CostEstimate(flops=0, bytes_accessed=8 * HELD * ROWS, transcendentals=0),
    )(keys, best, even_found, odd_found)


def local(embeddings, ranks, block_rows, pair_list, pair_count):
    pairs = pair_list.transpose(0, 2, 1)
    even_on, odd_on, keys = first_pieces(pairs, block_rows, ranks, embeddings)
    even_first, odd_first = exchanged(even_on, 0), exchanged(odd_on, 1)
    units, best, even_on, odd_on, flags = local_pairs(pairs, pair_count, embeddings, keys)
    even_last, odd_last = exchanged(even_on, 0), exchanged(odd_on, 1)
    even_guest, best, even_keys, even_flags = first_guests(0, flags, even_first, keys, units, best)
    odd_guest, best, odd_keys, odd_flags = first_guests(1, flags, odd_first, keys, units, best)
    even_guest, best = next_guests(0, 1, even_flags, even_last, even_keys, even_guest, keys, units, best)
    even_found = exchanged(even_guest, 0)
    odd_guest, best = next_guests(1, 1, odd_flags, odd_last, odd_keys, odd_guest, keys, units, best)
    odd_found = exchanged(odd_guest, 1)
    return combined(keys, best, even_found, odd_found)


def solution(mesh):
    in_specs = (
        P(AXES, None, None),
        P(AXES, None),
        P(AXES),
        P(AXES, None, None),
        P(AXES),
    )
    return jax.shard_map(local, mesh=mesh, in_specs=in_specs, out_specs=P(AXES, None), check_vma=False)
```

```python
import functools

import jax
import jax.numpy as jnp
from jax import lax
from jax.experimental import pallas as pl
from jax.experimental.pallas import tpu as pltpu
from jax.sharding import PartitionSpec as P

ROWS = 1024
DIM = 1024
HELD = 3
COLS = 256
LANES = 128
GROUPS = DIM // LANES
NOTE = 4 * GROUPS
CUTS = ((0, 640, 1024), (0, 640, 1024))
DIGIT = 128
DEAD = DIGIT**3 - 1
NONE = -1e30
AXES = ("blk", "grp")
SMEM = pl.BlockSpec(memory_space=pltpu.SMEM)
VMEM = pl.BlockSpec(memory_space=pltpu.VMEM)
HBM = pl.BlockSpec(memory_space=pltpu.HBM)


def exchanged(value, boundary):
    count = lax.axis_size(AXES)
    pairs = [(low, low + 1) for low in range(boundary, count - 1, 2)]
    return lax.ppermute(value, AXES, pairs + [(high, low) for low, high in pairs])


def odd_device():
    return lax.axis_index(AXES[-1]) % 2


def odd_after(boundary):
    return odd_device() if boundary else 1 - odd_device()


def cut_rows(boundary, index):
    return CUTS[boundary][index + 1] - CUTS[boundary][index]


def shaped(shape, dtype):
    return jax.ShapeDtypeStruct(shape, dtype)


def unit_rows(raw):
    values = raw.astype(jnp.float32)
    scaling = lax.rsqrt(jnp.sum(values * values, axis=-1, keepdims=True) + 1e-06)
    return (values * scaling).astype(jnp.bfloat16)


def normalize(raw, units, rows):
    def step(index, carry):
        first = pl.multiple_of(index * LANES, LANES)
        at = pl.ds(first, LANES)
        if raw.shape[-1] == DIM:
            values = raw[at, :]
        else:
            values = jnp.concatenate([raw[pl.ds(group * rows + first, LANES), :] for group in range(GROUPS)], axis=1)
        units[at, :] = unit_rows(values)
        return carry

    lax.fori_loop(0, rows // LANES, step, 0, unroll=2 if rows % (2 * LANES) == 0 else True)


def spread(keys_row):
    return jnp.broadcast_to(keys_row, (LANES, LANES)).T


def gathered(partial):
    return jnp.max(partial.T, axis=0, keepdims=True)


def shifted(found):
    return jnp.maximum(1.0 + found, 0.0)


def pair_tile(left_units, left_keys, right_units, right_keys):
    similarity = lax.dot_general(
        left_units, right_units, (((1,), (1,)), ((), ())), preferred_element_type=jnp.float32
    )
    rows, cols = similarity.shape
    left_best = None
    right_best = []
    for group in range(cols // LANES):
        part = similarity[:, group * LANES : (group + 1) * LANES]
        keys = right_keys[:, group * LANES : (group + 1) * LANES]
        for_left = jnp.where(keys < left_keys, part, NONE)
        left_best = for_left if left_best is None else jnp.maximum(left_best, for_left)
        for_right = jnp.where(left_keys < keys, part, NONE)
        right_best.append(jnp.max(for_right.reshape(rows // 8, 8, LANES), axis=0))
    return left_best, jnp.concatenate(right_best, axis=1)


def pair_strip(first, left_units, left_keys, left_acc, right_units, right_keys, right_acc, cols):
    rows = pl.ds(first, left_units.shape[0] - first)
    left_best, right_best = pair_tile(left_units[rows, :], left_keys[rows, :], right_units[cols, :], right_keys[:, cols])
    left_acc[rows, :] = jnp.maximum(left_acc[rows, :], left_best)
    right_acc[:, cols] = jnp.maximum(right_acc[:, cols], right_best)


def note_rows(keys, flags):
    keys = jnp.concatenate([keys[:, group * LANES : (group + 1) * LANES] for group in range(GROUPS)], axis=0)
    row = lax.broadcasted_iota(jnp.int32, keys.shape, 0)
    marks = jnp.zeros_like(keys)
    for index, flag in enumerate(flags):
        marks = jnp.where(row == index, flag, marks)
    note = jnp.concatenate([keys % DIGIT, (keys // DIGIT) % DIGIT, keys // DIGIT**2, marks], axis=0)
    return note.astype(jnp.float32).astype(jnp.bfloat16)


def noted(note):
    digits = note.astype(jnp.float32).astype(jnp.int32)
    low, middle, high, marks = (digits[part * GROUPS : (part + 1) * GROUPS] for part in range(4))
    keys = low + middle * DIGIT + high * DIGIT**2
    return jnp.concatenate([keys[group : group + 1] for group in range(GROUPS)], axis=1), marks


def piece_copies(items, raw, pieces, sems):
    odd, copies = odd_device(), []
    for (boundary, index), piece in zip(items, pieces):
        first, rows = CUTS[boundary][index], cut_rows(boundary, index)
        block = (HELD - 1) * (odd if boundary else 1 - odd)
        if index == 0:
            parts = [
                (raw.at[block, pl.ds(first, rows), pl.ds(group * LANES, LANES)], piece.at[pl.ds(group * rows, rows)])
                for group in range(GROUPS)
            ]
        else:
            parts = [(raw.at[block, pl.ds(first, rows)], piece)]
        for source, target in parts:
            copies.append(pltpu.make_async_copy(source, target, sems.at[len(copies)]))
    return copies


def boundary_flags(pairs):
    def listed(u, v):
        found = jnp.int32(0)
        for slot in range(pairs.shape[2]):
            found = found | ((pairs[0, 0, slot] == u) & (pairs[0, 1, slot] == v)).astype(jnp.int32)
        return found

    ahead, near, far = listed(HELD + 1, HELD - 1), listed(HELD, HELD - 1), listed(HELD, HELD - 2)
    here, there = ahead * near, (1 - ahead) * near
    return [here, ahead, there], [there, far, here]


def first_kernel(
    pairs_hbm, live_hbm, ranks_hbm, raw, even_on, odd_on, keys, pairs, live, ranks, sems, small_sems
):
    odd = odd_device()
    copies = piece_copies(((0, 0), (1, 0)), raw, (even_on, odd_on), sems)
    small = [
        pltpu.make_async_copy(source, target, small_sems.at[index])
        for index, (source, target) in enumerate(((pairs_hbm, pairs), (live_hbm, live), (ranks_hbm, ranks)))
    ]
    for copy in small + copies:
        copy.start()
    for copy in small:
        copy.wait()
    position = lax.broadcasted_iota(jnp.int32, (1, ROWS), 1)
    for block in range(HELD):
        keys[block : block + 1, :] = jnp.where(position < live[block], ranks[block : block + 1, :], DEAD)

    left_flags, right_flags = boundary_flags(pairs)
    note_last = note_rows(keys[HELD - 1 : HELD, :], [])
    note_first = note_rows(keys[0:1, :], right_flags)
    even_on[pl.ds(cut_rows(0, 0) * GROUPS, NOTE), :] = jnp.where(odd == 1, note_first, note_last)
    odd_on[pl.ds(cut_rows(1, 0) * GROUPS, NOTE), :] = jnp.where(odd == 1, note_last, note_first)
    for copy in copies:
        copy.wait()


def in_hbm(*values):
    return [pltpu.with_memory_space_constraint(value, pltpu.HBM) for value in values]


def first_pieces(pairs, live, ranks, raw):
    even, odd = (shaped((cut_rows(boundary, 0) * GROUPS + NOTE, LANES), jnp.bfloat16) for boundary in range(2))
    return pl.pallas_call(
        first_kernel,
        out_shape=(even, odd, shaped((HELD, ROWS), jnp.int32)),
        in_specs=[HBM] * 4,
        out_specs=(VMEM,) * 3,
        scratch_shapes=[
            pltpu.SMEM(pairs.shape, jnp.int32),
            pltpu.SMEM(live.shape, jnp.int32),
            pltpu.VMEM(ranks.shape, jnp.int32),
            pltpu.SemaphoreType.DMA((2 * GROUPS,)),
            pltpu.SemaphoreType.DMA((3,)),
        ],
        compiler_params=pltpu.CompilerParams(vmem_limit_bytes=6 << 20),
        cost_estimate=pl.CostEstimate(flops=0, bytes_accessed=4 * ROWS * DIM, transcendentals=0),
    )(*in_hbm(pairs, live, ranks, raw))


def local_kernel(pairs, count, raw, keys, units, best, even_on, odd_on, flags, spread_keys, left_acc, right_acc, sems):
    copies = piece_copies(((0, 1), (1, 1)), raw, (even_on, odd_on), sems)
    for copy in copies:
        copy.start()
    for index, flag in enumerate(boundary_flags(pairs)[0]):
        flags[index] = flag
    for block in range(HELD):
        for group in range(ROWS // LANES):
            rows = pl.ds(group * LANES, LANES)
            spread_keys[block, rows, :] = spread(keys[block : block + 1, rows])
        normalize(raw.at[block], units.at[block], ROWS)
    left_acc[...] = jnp.full_like(left_acc, NONE)
    right_acc[...] = jnp.full_like(right_acc, NONE)

    def visit(slot, carry):
        left, right = pairs[0, 0, slot] - HELD, pairs[0, 1, slot] - HELD

        def strip(first, col):
            pair_strip(
                first, units.at[left], spread_keys.at[left], left_acc.at[left],
                units.at[right], keys.at[pl.ds(right, 1)], right_acc.at[right], pl.ds(col, COLS),
            )

        @pl.when(right == left)
        def _():
            for col in range(0, ROWS, COLS):
                strip(col, col)

        @pl.when((right >= 0) & (right != left))
        def _():
            for col in range(0, ROWS, COLS):
                strip(0, col)

        return carry

    lax.fori_loop(0, count[0], visit, 0)
    for block in range(HELD):
        for group in range(ROWS // LANES):
            rows = pl.ds(group * LANES, LANES)
            found = jnp.maximum(
                gathered(left_acc[block, rows, :]),
                jnp.max(right_acc[block, :, rows], axis=0, keepdims=True),
            )
            best[block : block + 1, rows] = shifted(found)
    for copy in copies:
        copy.wait()


def local_pairs(pairs, count, raw, keys):
    even, odd = (shaped((cut_rows(boundary, 1), DIM), jnp.bfloat16) for boundary in range(2))
    return pl.pallas_call(
        local_kernel,
        out_shape=(
            shaped((HELD, ROWS, DIM), jnp.bfloat16),
            shaped((HELD, ROWS), jnp.float32),
            even,
            odd,
            shaped((3,), jnp.int32),
        ),
        in_specs=[SMEM, SMEM, VMEM, VMEM],
        out_specs=(VMEM,) * 4 + (SMEM,),
        scratch_shapes=[
            pltpu.VMEM((HELD, ROWS, LANES), jnp.int32),
            pltpu.VMEM((HELD, ROWS, LANES), jnp.float32),
            pltpu.VMEM((HELD, 8, ROWS), jnp.float32),
            pltpu.SemaphoreType.DMA((2,)),
        ],
        compiler_params=pltpu.CompilerParams(vmem_limit_bytes=24 << 20),
        cost_estimate=pl.CostEstimate(flops=2 * ROWS * ROWS * DIM, bytes_accessed=4 * HELD * ROWS * DIM, transcendentals=0),
    )(pairs, count, raw, keys)


def guest_pairs(boundary, index, flags, raw, guest_keys, keys, units, right_acc, guest_units, spread_keys, left_acc):
    first, rows = CUTS[boundary][index], cut_rows(boundary, index)
    guest_keys = guest_keys[:, first : first + rows]
    beside = (HELD - 1) * (odd_after(boundary))
    cols = max(COLS, COLS * ROWS // rows // COLS * COLS)
    left_acc[...] = jnp.full_like(left_acc, NONE)
    some_live = jnp.min(guest_keys[:, :LANES].astype(jnp.float32)) < DEAD
    takes_beside = flags[0] if index == 0 else jnp.int32(0)

    def meet(block, low, high, width):
        for col in range(low, high, width):
            pair_strip(
                0, guest_units, spread_keys, left_acc,
                units.at[block], keys.at[pl.ds(block, 1)], right_acc.at[block], pl.ds(col, width),
            )

    @pl.when(((takes_beside != 0) | (flags[1] != 0) | (flags[2] != 0)) & some_live)
    def _():
        normalize(raw, guest_units, rows)
        for group in range(rows // LANES):
            at = pl.ds(group * LANES, LANES)
            spread_keys[at, :] = spread(guest_keys[:, group * LANES : (group + 1) * LANES])

        def visit(which, carry):
            @pl.when(flags[which] != 0)
            def _():
                meet(jnp.where(which == 0, beside, 1), 0, ROWS, cols)

            return carry

        lax.fori_loop(0 if index == 0 else 1, 2, visit, 0)

        @pl.when(flags[2] != 0)
        def _():
            low = CUTS[boundary][-2]
            meet(beside, low, ROWS, ROWS - low)


def finish_guests(left_acc, first, guest_earlier, guest_best):
    if first:
        guest_best[:, pl.ds(0, first)] = guest_earlier[...]
    for group in range(left_acc.shape[0] // LANES):
        found = gathered(left_acc[pl.ds(group * LANES, LANES), :])
        guest_best[:, pl.ds(first + group * LANES, LANES)] = shifted(found)


def finish_held(right_acc, best_before, best):
    for block in range(HELD):
        found = jnp.max(right_acc[block], axis=0, keepdims=True)
        best[block : block + 1, :] = jnp.maximum(best_before[block : block + 1, :], shifted(found))


def guest_scratch(rows):
    return [
        pltpu.VMEM((HELD, 8, ROWS), jnp.float32),
        pltpu.VMEM((rows, DIM), jnp.bfloat16),
        pltpu.VMEM((rows, LANES), jnp.int32),
        pltpu.VMEM((rows, LANES), jnp.float32),
    ]


def guest_cost(rows):
    return pl.CostEstimate(flops=2 * rows * ROWS * DIM, bytes_accessed=2 * (rows + HELD * ROWS) * DIM, transcendentals=0)


def first_guests_kernel(
    boundary, flags, raw, keys, units, best_before, guest_best, best, guest_keys, guest_flags, right_acc, *scratch
):
    rows = cut_rows(boundary, 0)
    after = odd_after(boundary)
    right_acc[...] = jnp.full_like(right_acc, NONE)
    noted_keys, marks = noted(raw[pl.ds(rows * GROUPS, NOTE), :])
    guest_keys[...] = noted_keys
    for which in range(3):
        marked = (jnp.max(marks[which : which + 1, :].astype(jnp.float32)) > 0.5).astype(jnp.int32)
        guest_flags[which] = jnp.where(after == 1, marked, flags[which])
    guest_pairs(boundary, 0, guest_flags, raw, guest_keys, keys, units, right_acc, *scratch)
    finish_guests(scratch[-1], 0, None, guest_best)
    finish_held(right_acc, best_before, best)


def first_guests(boundary, flags, raw, keys, units, best_before):
    rows = cut_rows(boundary, 0)
    return pl.pallas_call(
        functools.partial(first_guests_kernel, boundary),
        out_shape=(
            shaped((1, rows), jnp.float32),
            shaped((HELD, ROWS), jnp.float32),
            shaped((1, ROWS), jnp.int32),
            shaped((3,), jnp.int32),
        ),
        in_specs=[SMEM] + [VMEM] * 4,
        out_specs=(VMEM, VMEM, VMEM, SMEM),
        scratch_shapes=guest_scratch(rows),
        compiler_params=pltpu.CompilerParams(vmem_limit_bytes=16 << 20),
        cost_estimate=guest_cost(rows),
    )(flags, raw, keys, units, best_before)


def next_guests_kernel(
    boundary, index, flags, raw, guest_keys, guest_earlier, keys, units, best_before, guest_best, best, right_acc, *scratch
):
    right_acc[...] = jnp.full_like(right_acc, NONE)
    guest_pairs(boundary, index, flags, raw, guest_keys, keys, units, right_acc, *scratch)
    finish_guests(scratch[-1], CUTS[boundary][index], guest_earlier, guest_best)
    finish_held(right_acc, best_before, best)


def next_guests(boundary, index, flags, *rest):
    rows = cut_rows(boundary, index)
    return pl.pallas_call(
        functools.partial(next_guests_kernel, boundary, index),
        out_shape=(shaped((1, CUTS[boundary][index + 1]), jnp.float32), shaped((HELD, ROWS), jnp.float32)),
        in_specs=[SMEM] + [VMEM] * len(rest),
        out_specs=(VMEM, VMEM),
        scratch_shapes=guest_scratch(rows),
        compiler_params=pltpu.CompilerParams(vmem_limit_bytes=16 << 20),
        cost_estimate=guest_cost(rows),
    )(flags, *rest)


def combined_kernel(keys, best_before, even_found, odd_found, best):
    odd = odd_device() == 1
    even, other = even_found[...], odd_found[...]
    found = (jnp.where(odd, even, other), jnp.zeros_like(even), jnp.where(odd, other, even))
    for block in range(HELD):
        rows = slice(block, block + 1)
        best[rows, :] = jnp.where(keys[rows, :] != DEAD, jnp.maximum(best_before[rows, :], found[block]), 0.0)


def combined(keys, best, even_found, odd_found):
    return pl.pallas_call(
        combined_kernel,
        out_shape=shaped((HELD, ROWS), jnp.float32),
        in_specs=[VMEM] * 4,
        out_specs=VMEM,
        compiler_params=pltpu.CompilerParams(vmem_limit_bytes=2 << 20),
        cost_estimate=pl.CostEstimate(flops=0, bytes_accessed=8 * HELD * ROWS, transcendentals=0),
    )(keys, best, even_found, odd_found)


def local(embeddings, ranks, block_rows, pair_list, pair_count):
    pairs = pair_list.transpose(0, 2, 1)
    even_on, odd_on, keys = first_pieces(pairs, block_rows, ranks, embeddings)
    even_first, odd_first = exchanged(even_on, 0), exchanged(odd_on, 1)
    units, best, even_on, odd_on, flags = local_pairs(pairs, pair_count, embeddings, keys)
    even_last, odd_last = exchanged(even_on, 0), exchanged(odd_on, 1)
    even_guest, best, even_keys, even_flags = first_guests(0, flags, even_first, keys, units, best)
    odd_guest, best, odd_keys, odd_flags = first_guests(1, flags, odd_first, keys, units, best)
    even_guest, best = next_guests(0, 1, even_flags, even_last, even_keys, even_guest, keys, units, best)
    even_found = exchanged(even_guest, 0)
    odd_guest, best = next_guests(1, 1, odd_flags, odd_last, odd_keys, odd_guest, keys, units, best)
    odd_found = exchanged(odd_guest, 1)
    return combined(keys, best, even_found, odd_found)


def solution(mesh):
    in_specs = (
        P(AXES, None, None),
        P(AXES, None),
        P(AXES),
        P(AXES, None, None),
        P(AXES),
    )
    return jax.shard_map(local, mesh=mesh, in_specs=in_specs, out_specs=P(AXES, None), check_vma=False)
```
